256 devices in a mesh: aux: 16 (over y_lo, x, core), blk: 16 (over y_hi, z).
Axes of the slice: x: 4, y: 4 (y_hi: 2, y_lo: 2; y = y_hi * 2 + y_lo), z: 8, core: 2. Of those that a mesh axis runs over, the one named last changes fastest.
Arguments:
- half_b: bfloat16 [32, 8192, 512], P('aux', 'blk'), may hold values from -1.25 to 1.25
Outputs:
- exchange: float32 [8192, 8192], P('blk', 'aux')
The draws below stay inside these ranges and needn't reach their ends.
All inputs are finite; a program needn't handle non-finite values.
Results may differ from the reference program's by a relative error of at most 0.0003.
Values may be sent and summed in bfloat16 or wider, within the bound.
No kernel may reach another device: no remote copies, remote signals or barrier semaphores. Data moves between devices by JAX's collectives and lax.ppermute only.
A program may use at most 128 MiB of HBM per device.

```python
import jax
import jax.numpy as jnp

NOCC = 512
MU_DEV = 512
NAUX = 32
NBF = 8192


def block_levels(rng, extent, split, low, top_value):
    factor_of = 1.0
    for axis_at, blocks in split:
        draws = jax.random.uniform(jax.random.fold_in(jax.random.fold_in(rng, 6), axis_at), (blocks,), jnp.float32, low / len(split), top_value / len(split))
        factor_of = factor_of * jnp.repeat(jnp.exp(draws), extent[axis_at] // blocks).reshape((-1,) + (1,) * (len(extent) - 1 - axis_at))
    return factor_of


def normal_values(stream_key, extent, scale, most, cuts=(), kind=jnp.bfloat16):
    factor_of = block_levels(stream_key, extent, cuts, -0.22, 0.18) if cuts else 1.0
    entries = jax.random.normal(stream_key, extent, jnp.float32) * scale * factor_of
    return jnp.minimum(jnp.maximum(entries, -most), most).astype(kind)


def setup_inputs(seed: int = 0) -> dict:
    key_of = jax.random.split(jax.random.key(seed), 2)
    return {
        "half_b": normal_values(key_of[0], (NAUX, NBF, NOCC), ((NAUX * NOCC) ** -0.25), 1.25, ((0, 16), (1, 16))),
    }


def reference(half_b):
    flat = jnp.transpose(half_b, (1, 0, 2)).reshape(NBF, NAUX * NOCC)
    full = jnp.dot(flat, flat.T, preferred_element_type=jnp.float32)
    blocks = jnp.arange(NBF, dtype=jnp.int32) // MU_DEV
    keep = blocks[:, None] <= blocks[None, :]
    return jnp.where(keep, full, jnp.float32(0.0))
```

```python
import functools

import jax
import jax.numpy as jnp
import numpy as np
from jax import lax
from jax.experimental import pallas as pl
from jax.experimental.pallas import tpu as pltpu
from jax.sharding import PartitionSpec as P

ALL = ("aux", "blk")
NX, NZ, GROUPS = 4, 8, 16
EMPTY = 63
VMEM_LIMIT = 48 * 2**20


def device(y_lo, x, core, blk):
    return ((y_lo * NX + x % NX) * 2 + core) * GROUPS + blk


def block(h, z):
    return h % 2 * NZ + z % NZ


def every(move):
    return [
        (device(*move(y_lo, x, core, h, z)), device(y_lo, x, core, block(h, z)))
        for y_lo in range(2)
        for x in range(NX)
        for core in range(2)
        for h in range(2)
        for z in range(NZ)
    ]


def send(value, pairs):
    return lax.ppermute(value, ALL, pairs)


O, PZ, MZ, Y0 = (0, 0), (0, 1), (0, -1), (1, 0)
PP, MM, Y1, Y2 = (0, 2), (0, -2), (1, 1), (1, 2)
HELD_A = (O, PZ, MZ, Y0)
HELD_B = (MZ, PZ, PP, MM, Y1)
HELD_C = (MM, Y2)


def units_of(held, pairs, h, z):
    found = []
    for at, (first, second, halves) in enumerate(pairs):
        i, j = block(h + first[0], z + first[1]), block(h + second[0], z + second[1])
        for half in halves(h, z):
            found.append(((at * 2 + (i > j)) * 2 + half, min(i, j), max(i, j), half))
    return found


def both(h, z):
    return (0, 1)


def by_h(h, z):
    return (h,)


def by_z(h, z):
    return (0,) if 2 <= z < 6 else (1,)


PAIRS_A = ((O, PZ, both), (MZ, PZ, both), (O, Y0, by_h), (MZ, Y0, both))
PAIRS_B = ((MM, PZ, both), (MM, PP, by_z), (MZ, Y1, both), (MM, Y1, both))
PAIRS_C = ((MM, Y2, by_h),)


def ring(a, b, n):
    return min((a - b) % n, (b - a) % n)


def hops(y_lo, x, core, h, z, row, col):
    y_at, y_to = h * 2 + y_lo, row // NZ * 2 + col // 8
    return ring(x, col // 2 % NX, NX) + ring(y_at, y_to, 4) + ring(z, row % NZ, NZ) + 0.1 * (core != col % 2)


def assign(units, y_lo, h, z):
    best = {0: (0.0, ())}
    for _, row, col, _ in units:
        grown = {}
        for mask, (cost, taken) in best.items():
            for place in range(8):
                if mask >> place & 1:
                    continue
                total = cost + hops(y_lo, place // 2, place % 2, h, z, row, col) ** 2
                key = mask | 1 << place
                if key not in grown or total < grown[key][0]:
                    grown[key] = (total, taken + (place,))
        best = grown
    return min(best.values())[1]


@functools.cache
def plan():
    tables = np.full((2, GROUPS, 2, NX), EMPTY, np.int32)
    code_c = np.zeros((GROUPS,), np.int32)
    target_c = {}
    final = {(batch, half): [] for batch in range(2) for half in range(2)}
    for h in range(2):
        for z in range(NZ):
            own = block(h, z)
            for batch in range(2):
                units = units_of(None, PAIRS_B if batch else PAIRS_A, h, z)
                count = len(units)
                if batch:
                    units += units_of(None, PAIRS_C, h, z)
                places = assign(units, batch, h, z)
                for at, (unit, place) in enumerate(zip(units, places)):
                    code, row, col, half = unit
                    x, core = place // 2, place % 2
                    if at < count:
                        tables[batch, own, core, x] = code
                    else:
                        code_c[own] = code
                        target_c[own] = (batch, x, core)
                    final[batch, half].append((device(batch, x, core, own), col * GROUPS + row))
    local = np.zeros((2, 16, GROUPS, 2, NX), np.int32)
    for aux in range(16):
        x, core = aux // 2 % NX, aux % 2
        for j in range(NX):
            local[:, aux, :, 0, j] = tables[:, :, core, (x + j) % NX]
            local[:, aux, :, 1, j] = tables[:, :, 1 - core, (x + j) % NX]
    target_d = {b: (b // 8, b // 2 % NX, b % 2) for b in range(GROUPS)}
    return local, code_c, target_c, target_d, final


def dot_t(a, b):
    return lax.dot_general(a, b, (((1,), (1,)), ((), ())), preferred_element_type=jnp.float32)


def half_product(rows, cols, half):
    at = pl.ds(pl.multiple_of(half * 256, 256), 256)
    total = dot_t(rows[0, at, :], cols[0])
    for k in range(1, rows.shape[0]):
        total += dot_t(rows[k, at, :], cols[k])
    return total


def units_kernel(index_pairs, table, *refs):
    held, out = refs[:-1], refs[-1]

    def slot(j, carry):
        code = table[j]
        half = code % 2
        for at, (first, second) in enumerate(index_pairs):

            @pl.when(code // 2 == at * 2)
            def _():
                out[j] = half_product(held[first], held[second], half)

            @pl.when(code // 2 == at * 2 + 1)
            def _():
                out[j] = half_product(held[second], held[first], half)

        @pl.when(code == EMPTY)
        def _():
            out[j] = jnp.zeros(out.shape[1:], jnp.float32)

        return carry

    lax.fori_loop(0, out.shape[0], slot, 0)


def products(table, held, names, pairs):
    index_pairs = tuple((names.index(a), names.index(b)) for a, b, _ in pairs)
    return pl.pallas_call(
        functools.partial(units_kernel, index_pairs),
        out_shape=jax.ShapeDtypeStruct((table.shape[0], 256, 512), jnp.float32),
        in_specs=[pl.BlockSpec(memory_space=pltpu.SMEM)]
        + [pl.BlockSpec(memory_space=pltpu.VMEM)] * len(held),
        out_specs=pl.BlockSpec(memory_space=pltpu.VMEM),
        compiler_params=pltpu.CompilerParams(vmem_limit_bytes=VMEM_LIMIT),
    )(table, *held)


def square_kernel(own, out):
    total = dot_t(own[0], own[0])
    for k in range(1, own.shape[0]):
        total += dot_t(own[k], own[k])
    out[...] = total


def square(own):
    return pl.pallas_call(
        square_kernel,
        out_shape=jax.ShapeDtypeStruct((own.shape[1],) * 2, jnp.float32),
        in_specs=[pl.BlockSpec(memory_space=pltpu.VMEM)],
        out_specs=pl.BlockSpec(memory_space=pltpu.VMEM),
        compiler_params=pltpu.CompilerParams(vmem_limit_bytes=VMEM_LIMIT),
    )(own)


def to_one(value, targets):
    def pairs(source, only):
        return [
            (device(*source(y, x, c), b), device(*only(y, x, c), b))
            for b, (y, x, c) in targets.items()
        ]

    middle = value.shape[0] // 2
    steps = [(y, dx) for y in range(2) for dx in range(NX)]
    across = [
        (device(y, tx + dx, 1 - tc, b), device(y, tx + dx, tc, b))
        for b, (_, tx, tc) in targets.items()
        for y, dx in steps
    ]
    value = value + send(value, across)

    def along(offset_from, offset_to):
        return [
            (device(y, tx + offset_from, tc, b), device(y, tx + offset_to, tc, b))
            for b, (_, tx, tc) in targets.items()
            for y in range(2)
        ]

    top = send(value[:middle], along(2, 1))
    bottom = send(value[middle:], along(2, 3))
    value = value + jnp.concatenate([top, bottom], 0)
    value = value + send(value, along(1, 0)) + send(value, along(3, 0))
    last = [(device(1 - ty, tx, tc, b), device(ty, tx, tc, b)) for b, (ty, tx, tc) in targets.items()]
    return value + send(value, last)


CORE_SWAP = every(lambda y, x, c, h, z: (y, x, 1 - c, block(h, z)))
FROM_LEFT = every(lambda y, x, c, h, z: (y, x - 1, c, block(h, z)))
FROM_RIGHT = every(lambda y, x, c, h, z: (y, x + 1, c, block(h, z)))
FROM_UP = every(lambda y, x, c, h, z: (y, x, c, block(h, z + 1)))
FROM_DOWN = every(lambda y, x, c, h, z: (y, x, c, block(h, z - 1)))
FROM_OTHER = every(lambda y, x, c, h, z: (y, x, c, block(h + 1, z)))


def reduced(keep, given, y_to):
    got = send(given, CORE_SWAP)
    middle = keep.shape[1] // 2
    far_top = send(keep[2, :middle] + got[2, :middle], FROM_LEFT)
    far_bottom = send(keep[2, middle:] + got[2, middle:], FROM_RIGHT)
    right = keep[1] + got[1]
    right = jnp.concatenate([right[:middle] + far_top, right[middle:]], 0)
    left = keep[3] + got[3]
    left = jnp.concatenate([left[:middle], left[middle:] + far_bottom], 0)
    total = keep[0] + got[0] + send(right, FROM_LEFT) + send(left, FROM_RIGHT)
    over = [
        (device(1 - y_to, x, core, b), device(y_to, x, core, b))
        for x in range(NX)
        for core in range(2)
        for b in range(GROUPS)
    ]
    return total + send(total, over)


def per_device(half_b):
    local, code_c, target_c, target_d, final = plan()
    aux, blk = lax.axis_index("aux"), lax.axis_index("blk")
    tables = jnp.asarray(local.transpose(1, 2, 0, 3, 4).reshape(256, 4, NX))[aux * GROUPS + blk]
    table_c = jnp.asarray(code_c)[blk].reshape(1)

    held = {O: half_b}
    held[PZ] = send(half_b, FROM_UP)
    held[MZ] = send(half_b, FROM_DOWN)
    held[Y0] = send(half_b, FROM_OTHER)
    diagonal = to_one(square(half_b), target_d)

    held[PP] = send(held[PZ], FROM_UP)
    held[MM] = send(held[MZ], FROM_DOWN)
    held[Y1] = send(held[PZ], FROM_OTHER)

    names = HELD_A
    have = [held[n] for n in names]
    given = products(tables[1], have, names, PAIRS_A)
    keep = products(tables[0], have, names, PAIRS_A)
    done_a = reduced(keep, given, 0)
    top = send(done_a, final[0, 0])
    bottom = send(done_a, final[0, 1])

    held[Y2] = send(held[PP], FROM_OTHER)
    names = HELD_B
    have = [held[n] for n in names]
    given = products(tables[3], have, names, PAIRS_B)
    keep = products(tables[2], have, names, PAIRS_B)
    done_b = reduced(keep, given, 1)

    done_c = products(table_c, [held[n] for n in HELD_C], HELD_C, PAIRS_C)
    done_c = to_one(done_c[0], target_c)
    place_c = np.zeros((GROUPS,), np.int32)
    for b, (y, x, core) in target_c.items():
        place_c[b] = (y * NX + x) * 2 + core
    done_b = jnp.where(aux == jnp.asarray(place_c)[blk], done_c, done_b)
    top = top + send(done_b, final[1, 0])
    bottom = bottom + send(done_b, final[1, 1])
    other = jnp.concatenate([top, bottom], 0)
    return jnp.where(aux == blk, diagonal, other)


def solution(mesh):
    placed = (P("aux", "blk", None),)
    return jax.shard_map(
        per_device, mesh=mesh, in_specs=placed, out_specs=P("blk", "aux"), check_vma=False
    )
```

```python
import functools

import jax
import jax.numpy as jnp
import numpy as np
from jax import lax
from jax.experimental import pallas as pl
from jax.experimental.pallas import tpu as pltpu
from jax.sharding import PartitionSpec as P

ALL = ("aux", "blk")
NX, NZ, GROUPS = 4, 8, 16
VMEM_LIMIT = 16 * 2**20


def device(y_lo, x, core, blk):
    return ((y_lo * NX + x % NX) * 2 + core) * GROUPS + blk


def block(h, z):
    return h % 2 * NZ + z % NZ


def every(move):
    return [
        (device(*move(y_lo, x, core, h, z)), device(y_lo, x, core, block(h, z)))
        for y_lo in range(2)
        for x in range(NX)
        for core in range(2)
        for h in range(2)
        for z in range(NZ)
    ]


def send(value, pairs):
    return lax.ppermute(value, ALL, pairs)


O, PZ, MZ, Y0 = (0, 0), (0, 1), (0, -1), (1, 0)
PP, MM, Y1, Y2 = (0, 2), (0, -2), (1, 1), (1, 2)
HELD_A = (O, PZ, MZ, Y0)
HELD_B = (O, MZ, PZ, PP, MM, Y1)
HELD_C = (MM, Y2)


def units_of(pairs, h, z):
    found = []
    for at, (first, second, halves) in enumerate(pairs):
        i, j = block(h + first[0], z + first[1]), block(h + second[0], z + second[1])
        for half in halves(h, z):
            found.append(((at * 2 + (i > j)) * 2 + half, min(i, j), max(i, j), half))
    return found


def both(h, z):
    return (0, 1)


def by_h(h, z):
    return (h,)


def by_z(h, z):
    return (0,) if 2 <= z < 6 else (1,)


def upper(h, z):
    return (0,)


def lower(h, z):
    return (1,)


PAIRS_A = ((O, PZ, both), (MZ, PZ, both), (O, Y0, by_h), (MZ, Y0, both), (O, O, upper))
PAIRS_B = ((MM, PZ, both), (MM, PP, by_z), (MZ, Y1, both), (MM, Y1, both), (O, O, lower))
PAIRS_C = ((MM, Y2, by_h),)


def ring(a, b, n):
    return min((a - b) % n, (b - a) % n)


def hops(y_lo, x, core, h, z, row, col):
    y_at, y_to = h * 2 + y_lo, row // NZ * 2 + col // 8
    return ring(x, col // 2 % NX, NX) + ring(y_at, y_to, 4) + ring(z, row % NZ, NZ) + 0.1 * (core != col % 2)


def assign(units, y_lo, h, z):
    best = {0: (0.0, ())}
    for _, row, col, _ in units:
        grown = {}
        for mask, (cost, taken) in best.items():
            for place in range(8):
                if mask >> place & 1:
                    continue
                total = cost + hops(y_lo, place // 2, place % 2, h, z, row, col) ** 2
                key = mask | 1 << place
                if key not in grown or total < grown[key][0]:
                    grown[key] = (total, taken + (place,))
        best = grown
    return min(best.values())[1]


@functools.cache
def plan():
    tables = np.zeros((2, GROUPS, 2, NX), np.int32)
    code_c = np.zeros((GROUPS,), np.int32)
    target_c = {}
    final = {(batch, half): [] for batch in range(3) for half in range(2)}
    for h in range(2):
        for z in range(NZ):
            own = block(h, z)
            for batch in range(2):
                units = units_of(PAIRS_B if batch else PAIRS_A, h, z)
                for (code, row, col, half), place in zip(units, assign(units, batch, h, z)):
                    x, core = place // 2, place % 2
                    tables[batch, own, core, x] = code
                    final[batch, half].append((device(batch, x, core, own), col * GROUPS + row))
            ((code, row, col, half),) = units_of(PAIRS_C, h, z)
            code_c[own] = code
            target_c[own] = (col // 8, col // 2 % NX, col % 2)
            final[2, half].append((device(*target_c[own], own), col * GROUPS + row))
    local = np.zeros((2, 16, GROUPS, 2, NX), np.int32)
    for aux in range(16):
        x, core = aux // 2 % NX, aux % 2
        for j in range(NX):
            local[:, aux, :, 0, j] = tables[:, :, core, (x + j) % NX]
            local[:, aux, :, 1, j] = tables[:, :, 1 - core, (x + j) % NX]
    return local.reshape(2, 16 * GROUPS, 2 * NX), code_c, target_c, final


def dot_t(a, b):
    return lax.dot_general(a, b, (((1,), (1,)), ((), ())), preferred_element_type=jnp.float32)


def half_product(rows, cols, half):
    at = pl.ds(pl.multiple_of(half * 256, 256), 256)
    total = dot_t(rows[0, at, :], cols[0])
    for k in range(1, rows.shape[0]):
        total += dot_t(rows[k, at, :], cols[k])
    return total


def units_kernel(index_pairs, spare, table, *refs):
    held, outs = refs[: len(refs) - spare], refs[len(refs) - spare :]

    def slot(base, out, j, carry):
        code = table[base + j]
        half = code % 2
        for at, (first, second) in enumerate(index_pairs):

            @pl.when(code // 2 == at * 2)
            def _():
                out[j] = half_product(held[first], held[second], half)

            if first != second:

                @pl.when(code // 2 == at * 2 + 1)
                def _():
                    out[j] = half_product(held[second], held[first], half)

        return carry

    base = 0
    for out in outs:
        lax.fori_loop(0, out.shape[0], functools.partial(slot, base, out), 0)
        base += out.shape[0]


def products(table, held, names, pairs, counts):
    index_pairs = tuple((names.index(a), names.index(b)) for a, b, _ in pairs)
    return pl.pallas_call(
        functools.partial(units_kernel, index_pairs, len(counts)),
        out_shape=[pltpu.VMEM((count, 256, 512), jnp.float32) for count in counts],
        in_specs=[pl.BlockSpec(memory_space=pltpu.SMEM)]
        + [pl.BlockSpec(memory_space=pltpu.VMEM)] * len(held),
        out_specs=[pl.BlockSpec(memory_space=pltpu.VMEM)] * len(counts),
        compiler_params=pltpu.CompilerParams(vmem_limit_bytes=VMEM_LIMIT),
    )(table, *held)


def to_one(value, targets):
    def pairs(source, only):
        return [
            (device(*source(y, x, c), b), device(*only(y, x, c), b))
            for b, (y, x, c) in targets.items()
        ]

    middle = value.shape[0] // 2
    steps = [(y, dx) for y in range(2) for dx in range(NX)]
    across = [
        (device(y, tx + dx, 1 - tc, b), device(y, tx + dx, tc, b))
        for b, (_, tx, tc) in targets.items()
        for y, dx in steps
    ]
    value = value + send(value, across)

    def along(offset_from, offset_to):
        return [
            (device(y, tx + offset_from, tc, b), device(y, tx + offset_to, tc, b))
            for b, (_, tx, tc) in targets.items()
            for y in range(2)
        ]

    top = send(value[:middle], along(2, 1))
    bottom = send(value[middle:], along(2, 3))
    value = value + jnp.concatenate([top, bottom], 0)
    value = value + send(value, along(1, 0)) + send(value, along(3, 0))
    last = [(device(1 - ty, tx, tc, b), device(ty, tx, tc, b)) for b, (ty, tx, tc) in targets.items()]
    return value + send(value, last)


CORE_SWAP = every(lambda y, x, c, h, z: (y, x, 1 - c, block(h, z)))
FROM_LEFT = every(lambda y, x, c, h, z: (y, x - 1, c, block(h, z)))
FROM_RIGHT = every(lambda y, x, c, h, z: (y, x + 1, c, block(h, z)))
FROM_UP = every(lambda y, x, c, h, z: (y, x, c, block(h, z + 1)))
FROM_DOWN = every(lambda y, x, c, h, z: (y, x, c, block(h, z - 1)))
FROM_OTHER = every(lambda y, x, c, h, z: (y, x, c, block(h + 1, z)))


def near(keep, got):
    middle = keep.shape[1] // 2
    far_top = send(keep[2, :middle] + got[2, :middle], FROM_LEFT)
    far_bottom = send(keep[2, middle:] + got[2, middle:], FROM_RIGHT)
    right = keep[1] + got[1]
    right = jnp.concatenate([right[:middle] + far_top, right[middle:]], 0)
    left = keep[3] + got[3]
    left = jnp.concatenate([left[:middle], left[middle:] + far_bottom], 0)
    return keep[0] + got[0], right, left


def over_y(total, y_to):
    pairs = [
        (device(1 - y_to, x, core, b), device(y_to, x, core, b))
        for x in range(NX)
        for core in range(2)
        for b in range(GROUPS)
    ]
    return total + send(total, pairs)


def together(*values):
    return lax.optimization_barrier(values)


def per_device(half_b):
    local, code_c, target_c, final = plan()
    aux, blk = lax.axis_index("aux"), lax.axis_index("blk")
    place = aux * GROUPS + blk
    table_a, table_b = jnp.asarray(local[0])[place], jnp.asarray(local[1])[place]
    table_c = jnp.asarray(code_c)[blk].reshape(1)

    held = {O: half_b}
    held[PZ] = send(half_b, FROM_UP)
    held[MZ] = send(half_b, FROM_DOWN)
    held[Y0] = send(half_b, FROM_OTHER)

    held[PP] = send(held[PZ], FROM_UP)
    held[MM] = send(held[MZ], FROM_DOWN)
    held[Y1] = send(held[PZ], FROM_OTHER)

    have = [held[n] for n in HELD_A]
    keep, given = products(table_a, have, HELD_A, PAIRS_A, (NX, NX))
    own_a, right_a, left_a = near(keep, send(given, CORE_SWAP))
    from_left, from_right = send(right_a, FROM_LEFT), send(left_a, FROM_RIGHT)
    held[PP], held[MM], held[Y1], _, _ = together(held[PP], held[MM], held[Y1], right_a, left_a)

    held[Y2] = send(held[PP], FROM_OTHER)
    have = [held[n] for n in HELD_B]
    keep, given = products(table_b, have, HELD_B, PAIRS_B, (NX, NX))
    own_b, right_b, left_b = near(keep, send(given, CORE_SWAP))
    done_a = over_y(own_a + from_left + from_right, 0)
    right_b, left_b, _ = together(right_b, left_b, done_a)
    top = send(done_a, final[0, 0])
    bottom = send(done_a, final[0, 1])
    total_b = own_b + send(right_b, FROM_LEFT) + send(left_b, FROM_RIGHT)

    held[Y2], _, _ = together(held[Y2], right_b, left_b)
    (part_c,) = products(table_c, [held[n] for n in HELD_C], HELD_C, PAIRS_C, (1,))
    done_c = to_one(part_c[0], target_c)
    total_b, top, bottom = together(total_b, top, bottom)
    done_b = over_y(total_b, 1)
    top = top + send(done_b, final[1, 0]) + send(done_c, final[2, 0])
    bottom = bottom + send(done_b, final[1, 1]) + send(done_c, final[2, 1])
    return jnp.concatenate([top, bottom], 0)


def solution(mesh):
    placed = (P("aux", "blk", None),)
    return jax.shard_map(
        per_device, mesh=mesh, in_specs=placed, out_specs=P("blk", "aux"), check_vma=False
    )
```

```python
import functools

import jax
import jax.numpy as jnp
import numpy as np
from jax import lax
from jax.experimental import pallas as pl
from jax.experimental.pallas import tpu as pltpu
from jax.sharding import PartitionSpec as P

ALL = ("aux", "blk")
NX, NZ, GROUPS = 4, 8, 16
VMEM_LIMIT = 16 * 2**20


def device(y_lo, x, core, blk):
    return ((y_lo * NX + x % NX) * 2 + core) * GROUPS + blk


def block(h, z):
    return h % 2 * NZ + z % NZ


def every(move):
    return [
        (device(*move(y_lo, x, core, h, z)), device(y_lo, x, core, block(h, z)))
        for y_lo in range(2)
        for x in range(NX)
        for core in range(2)
        for h in range(2)
        for z in range(NZ)
    ]


def send(value, pairs):
    return lax.ppermute(value, ALL, pairs)


O, PZ, MZ, Y0 = (0, 0), (0, 1), (0, -1), (1, 0)
PP, MM, Y1, Y2 = (0, 2), (0, -2), (1, 1), (1, 2)
HELD_A = (O, PZ, MZ, Y0)
HELD_B = (O, MZ, PZ, PP, MM, Y1)
HELD_C = (MM, Y2)


def units_of(pairs, h, z):
    found = []
    for at, (first, second, halves) in enumerate(pairs):
        i, j = block(h + first[0], z + first[1]), block(h + second[0], z + second[1])
        for half in halves(h, z):
            found.append(((at * 2 + (i > j)) * 2 + half, min(i, j), max(i, j), half))
    return found


def both(h, z):
    return (0, 1)


def by_h(h, z):
    return (h,)


def by_z(h, z):
    return (0,) if 2 <= z < 6 else (1,)


def upper(h, z):
    return (0,)


def lower(h, z):
    return (1,)


PAIRS_A = ((O, PZ, both), (MZ, PZ, both), (O, Y0, by_h), (MZ, Y0, both), (O, O, upper))
PAIRS_B = ((MM, PZ, both), (MM, PP, by_z), (MZ, Y1, both), (MM, Y1, both), (O, O, lower))
PAIRS_C = ((MM, Y2, by_h),)


def ring(a, b, n):
    return min((a - b) % n, (b - a) % n)


def hops(y_lo, x, core, h, z, row, col):
    y_at, y_to = h * 2 + y_lo, row // NZ * 2 + col // 8
    return ring(x, col // 2 % NX, NX) + ring(y_at, y_to, 4) + ring(z, row % NZ, NZ) + 0.1 * (core != col % 2)


def assign(units, y_lo, h, z):
    best = {0: (0.0, ())}
    for _, row, col, _ in units:
        grown = {}
        for mask, (cost, taken) in best.items():
            for place in range(8):
                if mask >> place & 1:
                    continue
                total = cost + hops(y_lo, place // 2, place % 2, h, z, row, col) ** 2
                key = mask | 1 << place
                if key not in grown or total < grown[key][0]:
                    grown[key] = (total, taken + (place,))
        best = grown
    return min(best.values())[1]


@functools.cache
def plan():
    tables = np.zeros((2, GROUPS, 2, NX), np.int32)
    code_c = np.zeros((GROUPS,), np.int32)
    target_c = {}
    final = {(batch, half): [] for batch in range(3) for half in range(2)}
    for h in range(2):
        for z in range(NZ):
            own = block(h, z)
            for batch in range(2):
                units = units_of(PAIRS_B if batch else PAIRS_A, h, z)
                for (code, row, col, half), place in zip(units, assign(units, batch, h, z)):
                    x, core = place // 2, place % 2
                    tables[batch, own, core, x] = code
                    final[batch, half].append((device(batch, x, core, own), col * GROUPS + row))
            ((code, row, col, half),) = units_of(PAIRS_C, h, z)
            code_c[own] = code
            target_c[own] = (col // 8, col // 2 % NX, col % 2)
            final[2, half].append((device(*target_c[own], own), col * GROUPS + row))
    local = np.zeros((2, 16, GROUPS, 2, NX), np.int32)
    for aux in range(16):
        x, core = aux // 2 % NX, aux % 2
        for j in range(NX):
            local[:, aux, :, 0, j] = tables[:, :, core, (x + j) % NX]
            local[:, aux, :, 1, j] = tables[:, :, 1 - core, (x + j) % NX]
    return local.reshape(2, 16 * GROUPS, 2 * NX), code_c, target_c, final


def dot_t(a, b):
    return lax.dot_general(a, b, (((1,), (1,)), ((), ())), preferred_element_type=jnp.float32)


def half_product(rows, cols, half):
    at = pl.ds(pl.multiple_of(half * 256, 256), 256)
    total = dot_t(rows[0, at, :], cols[0])
    for k in range(1, rows.shape[0]):
        total += dot_t(rows[k, at, :], cols[k])
    return total


def units_kernel(index_pairs, spare, table, *refs):
    held, outs = refs[: len(refs) - spare], refs[len(refs) - spare :]

    def slot(base, out, j, carry):
        code = table[base + j]
        half = code % 2
        for at, (first, second) in enumerate(index_pairs):

            @pl.when(code // 2 == at * 2)
            def _():
                out[j] = half_product(held[first], held[second], half)

            if first != second:

                @pl.when(code // 2 == at * 2 + 1)
                def _():
                    out[j] = half_product(held[second], held[first], half)

        return carry

    base = 0
    for out in outs:
        lax.fori_loop(0, out.shape[0], functools.partial(slot, base, out), 0)
        base += out.shape[0]


def products(table, held, names, pairs, counts):
    index_pairs = tuple((names.index(a), names.index(b)) for a, b, _ in pairs)
    return pl.pallas_call(
        functools.partial(units_kernel, index_pairs, len(counts)),
        out_shape=[pltpu.VMEM((count, 256, 512), jnp.float32) for count in counts],
        in_specs=[pl.BlockSpec(memory_space=pltpu.SMEM)]
        + [pl.BlockSpec(memory_space=pltpu.VMEM)] * len(held),
        out_specs=[pl.BlockSpec(memory_space=pltpu.VMEM)] * len(counts),
        compiler_params=pltpu.CompilerParams(vmem_limit_bytes=VMEM_LIMIT),
    )(table, *held)


def toward(targets, source, only):
    return [
        (device(*source(y, x, c, step), b), device(*only(y, x, c, step), b))
        for b, (y, x, c) in targets.items()
        for step in range(8)
    ]


def one_core(value, targets):
    def at(core_of):
        return lambda y, x, c, step: (step // NX, x + step % NX, core_of(c))

    return value + send(value, toward(targets, at(lambda c: 1 - c), at(lambda c: c)))


def along(targets, offset_from, offset_to):
    def at(offset):
        return lambda y, x, c, step: (step % 2, x + offset, c)

    return sorted(set(toward(targets, at(offset_from), at(offset_to))))


def one_far(value, targets):
    middle = value.shape[0] // 2
    top = send(value[:middle], along(targets, 2, 1))
    bottom = send(value[middle:], along(targets, 2, 3))
    return value + jnp.concatenate([top, bottom], 0)


def one_near(value, targets):
    return value + send(value, along(targets, 1, 0)) + send(value, along(targets, 3, 0))


def one_y(value, targets):
    pairs = [(device(1 - y, x, c, b), device(y, x, c, b)) for b, (y, x, c) in targets.items()]
    return value + send(value, pairs)


CORE_SWAP = every(lambda y, x, c, h, z: (y, x, 1 - c, block(h, z)))
FROM_LEFT = every(lambda y, x, c, h, z: (y, x - 1, c, block(h, z)))
FROM_RIGHT = every(lambda y, x, c, h, z: (y, x + 1, c, block(h, z)))
FROM_UP = every(lambda y, x, c, h, z: (y, x, c, block(h, z + 1)))
FROM_DOWN = every(lambda y, x, c, h, z: (y, x, c, block(h, z - 1)))
FROM_OTHER = every(lambda y, x, c, h, z: (y, x, c, block(h + 1, z)))


def near(keep, got):
    middle = keep.shape[1] // 2
    far_top = send(keep[2, :middle] + got[2, :middle], FROM_LEFT)
    far_bottom = send(keep[2, middle:] + got[2, middle:], FROM_RIGHT)
    right = keep[1] + got[1]
    right = jnp.concatenate([right[:middle] + far_top, right[middle:]], 0)
    left = keep[3] + got[3]
    left = jnp.concatenate([left[:middle], left[middle:] + far_bottom], 0)
    return keep[0] + got[0], right, left


def over_y(total, y_to):
    pairs = [
        (device(1 - y_to, x, core, b), device(y_to, x, core, b))
        for x in range(NX)
        for core in range(2)
        for b in range(GROUPS)
    ]
    return total + send(total, pairs)


def together(*values):
    return lax.optimization_barrier(values)


def per_device(half_b):
    local, code_c, target_c, final = plan()
    aux, blk = lax.axis_index("aux"), lax.axis_index("blk")
    place = aux * GROUPS + blk
    table_a, table_b = jnp.asarray(local[0])[place], jnp.asarray(local[1])[place]
    table_c = jnp.asarray(code_c)[blk].reshape(1)

    held = {O: half_b}
    held[PZ] = send(half_b, FROM_UP)
    held[MZ] = send(half_b, FROM_DOWN)
    held[Y0] = send(half_b, FROM_OTHER)
    held[PZ], held[MZ], held[Y0] = together(held[PZ], held[MZ], held[Y0])

    held[PP] = send(held[PZ], FROM_UP)
    held[MM] = send(held[MZ], FROM_DOWN)
    held[Y1] = send(held[PZ], FROM_OTHER)
    keep, given = products(table_a, [held[n] for n in HELD_A], HELD_A, PAIRS_A, (NX, NX))
    own_a, right_a, left_a = near(keep, send(given, CORE_SWAP))
    own_a, right_a, left_a, held[PP], held[MM], held[Y1] = together(
        own_a, right_a, left_a, held[PP], held[MM], held[Y1]
    )

    held[Y2] = send(held[PP], FROM_OTHER)
    total_a = own_a + send(right_a, FROM_LEFT) + send(left_a, FROM_RIGHT)
    keep, given = products(table_b, [held[n] for n in HELD_B], HELD_B, PAIRS_B, (NX, NX))
    own_b, right_b, left_b = near(keep, send(given, CORE_SWAP))
    total_a, own_b, right_b, left_b, held[Y2] = together(total_a, own_b, right_b, left_b, held[Y2])

    done_a = over_y(total_a, 0)
    total_b = own_b + send(right_b, FROM_LEFT) + send(left_b, FROM_RIGHT)
    (part_c,) = products(table_c, [held[n] for n in HELD_C], HELD_C, PAIRS_C, (1,))
    part_c = one_far(one_core(part_c[0], target_c), target_c)
    done_a, total_b, part_c = together(done_a, total_b, part_c)

    top = send(done_a, final[0, 0])
    bottom = send(done_a, final[0, 1])
    done_b = over_y(total_b, 1)
    done_c = one_y(one_near(part_c, target_c), target_c)
    top, bottom, done_b, done_c = together(top, bottom, done_b, done_c)

    top = top + send(done_b, final[1, 0]) + send(done_c, final[2, 0])
    bottom = bottom + send(done_b, final[1, 1]) + send(done_c, final[2, 1])
    return jnp.concatenate([top, bottom], 0)


def solution(mesh):
    placed = (P("aux", "blk", None),)
    return jax.shard_map(
        per_device, mesh=mesh, in_specs=placed, out_specs=P("blk", "aux"), check_vma=False
    )
```

```python
import functools

import jax
import jax.numpy as jnp
import numpy as np
from jax import lax
from jax.experimental import pallas as pl
from jax.experimental.pallas import tpu as pltpu
from jax.sharding import PartitionSpec as P

ALL = ("aux", "blk")
NX, NZ, GROUPS = 4, 8, 16
VMEM_LIMIT = 16 * 2**20


def device(y_lo, x, core, blk):
    return ((y_lo * NX + x % NX) * 2 + core) * GROUPS + blk


def block(h, z):
    return h % 2 * NZ + z % NZ


def every(move):
    return [
        (device(*move(y_lo, x, core, h, z)), device(y_lo, x, core, block(h, z)))
        for y_lo in range(2)
        for x in range(NX)
        for core in range(2)
        for h in range(2)
        for z in range(NZ)
    ]


def send(value, pairs):
    return lax.ppermute(value, ALL, pairs)


O, PZ, MZ, Y0 = (0, 0), (0, 1), (0, -1), (1, 0)
PP, MM, Y1, Y2 = (0, 2), (0, -2), (1, 1), (1, 2)
HELD_A = (O, PZ, MZ, Y0)
HELD_B = (O, MZ, PZ, PP, MM, Y1)
HELD_C = (MM, Y2)


def units_of(pairs, h, z):
    found = []
    for at, (first, second, halves) in enumerate(pairs):
        i, j = block(h + first[0], z + first[1]), block(h + second[0], z + second[1])
        for half in halves(h, z):
            found.append(((at * 2 + (i > j)) * 2 + half, min(i, j), max(i, j), half))
    return found


def both(h, z):
    return (0, 1)


def by_h(h, z):
    return (h,)


def by_z(h, z):
    return (0,) if 2 <= z < 6 else (1,)


def upper(h, z):
    return (0,)


def lower(h, z):
    return (1,)


PAIRS_A = ((O, PZ, both), (MZ, PZ, both), (O, Y0, by_h), (MZ, Y0, both), (O, O, upper))
PAIRS_B = ((MM, PZ, both), (MM, PP, by_z), (MZ, Y1, both), (MM, Y1, both), (O, O, lower))
PAIRS_C = ((MM, Y2, by_h),)


def ring(a, b, n):
    return min((a - b) % n, (b - a) % n)


def assign(units):
    best = {0: (0.0, ())}
    for _, _, col, _ in units:
        grown = {}
        for mask, (cost, taken) in best.items():
            for place in range(8):
                if mask >> place & 1:
                    continue
                total = cost + ring(place // 2, col // 2 % NX, NX) ** 2 + 0.1 * (place % 2 != col % 2)
                key = mask | 1 << place
                if key not in grown or total < grown[key][0]:
                    grown[key] = (total, taken + (place,))
        best = grown
    return min(best.values())[1]


def plane(h, row, col):
    return h if row // NZ == col // NZ else 1 - h


@functools.cache
def plan():
    tables = np.zeros((2, GROUPS, 2, NX), np.int32)
    code_c = np.zeros((GROUPS,), np.int32)
    target_c = {}
    over = {0: [], 1: []}
    final = {(batch, half): [] for batch in range(3) for half in range(2)}
    for h in range(2):
        for z in range(NZ):
            own = block(h, z)
            for batch in range(2):
                units = units_of(PAIRS_B if batch else PAIRS_A, h, z)
                for (code, row, col, half), place in zip(units, assign(units)):
                    x, core, y = place // 2, place % 2, plane(h, row, col)
                    tables[batch, own, core, x] = code
                    over[batch].append((device(1 - y, x, core, own), device(y, x, core, own)))
                    final[batch, half].append((device(y, x, core, own), col * GROUPS + row))
            ((code, row, col, half),) = units_of(PAIRS_C, h, z)
            code_c[own] = code
            target_c[own] = (1 - h, col // 2 % NX, col % 2)
            final[2, half].append((device(*target_c[own], own), col * GROUPS + row))
    local = np.zeros((2, 16, GROUPS, 2, NX), np.int32)
    for aux in range(16):
        x, core = aux // 2 % NX, aux % 2
        for j in range(NX):
            local[:, aux, :, 0, j] = tables[:, :, core, (x + j) % NX]
            local[:, aux, :, 1, j] = tables[:, :, 1 - core, (x + j) % NX]
    return local.reshape(2, 16 * GROUPS, 2 * NX), code_c, target_c, over, final


def dot_t(a, b):
    return lax.dot_general(a, b, (((1,), (1,)), ((), ())), preferred_element_type=jnp.float32)


def half_product(rows, cols, half):
    at = pl.ds(pl.multiple_of(half * 256, 256), 256)
    total = dot_t(rows[0, at, :], cols[0])
    for k in range(1, rows.shape[0]):
        total += dot_t(rows[k, at, :], cols[k])
    return total


def units_kernel(index_pairs, spare, table, *refs):
    held, outs = refs[: len(refs) - spare], refs[len(refs) - spare :]

    def slot(base, out, j, carry):
        code = table[base + j]
        half = code % 2
        for at, (first, second) in enumerate(index_pairs):

            @pl.when(code // 2 == at * 2)
            def _():
                out[j] = half_product(held[first], held[second], half)

            if first != second:

                @pl.when(code // 2 == at * 2 + 1)
                def _():
                    out[j] = half_product(held[second], held[first], half)

        return carry

    base = 0
    for out in outs:
        lax.fori_loop(0, out.shape[0], functools.partial(slot, base, out), 0)
        base += out.shape[0]


def products(table, held, names, pairs, counts):
    index_pairs = tuple((names.index(a), names.index(b)) for a, b, _ in pairs)
    return pl.pallas_call(
        functools.partial(units_kernel, index_pairs, len(counts)),
        out_shape=[pltpu.VMEM((count, 256, 512), jnp.float32) for count in counts],
        in_specs=[pl.BlockSpec(memory_space=pltpu.SMEM)]
        + [pl.BlockSpec(memory_space=pltpu.VMEM)] * len(held),
        out_specs=[pl.BlockSpec(memory_space=pltpu.VMEM)] * len(counts),
        compiler_params=pltpu.CompilerParams(vmem_limit_bytes=VMEM_LIMIT),
    )(table, *held)


def toward(targets, source, only):
    return [
        (device(*source(y, x, c, step), b), device(*only(y, x, c, step), b))
        for b, (y, x, c) in targets.items()
        for step in range(8)
    ]


def copy_kernel(source, out):
    out[...] = source[...]


def placed(value):
    return pl.pallas_call(
        copy_kernel,
        out_shape=pltpu.VMEM(value.shape, value.dtype),
        in_specs=[pl.BlockSpec(memory_space=pltpu.VMEM)],
        out_specs=pl.BlockSpec(memory_space=pltpu.VMEM),
        compiler_params=pltpu.CompilerParams(vmem_limit_bytes=VMEM_LIMIT),
    )(value)


def one_core(value, targets):
    def at(core_of):
        return lambda y, x, c, step: (step // NX, x + step % NX, core_of(c))

    return value + send(value, toward(targets, at(lambda c: 1 - c), at(lambda c: c)))


def along(targets, offset_from, offset_to):
    def at(offset):
        return lambda y, x, c, step: (step % 2, x + offset, c)

    return sorted(set(toward(targets, at(offset_from), at(offset_to))))


def one_far(value, targets):
    middle = value.shape[0] // 2
    top = send(value[:middle], along(targets, 2, 1))
    bottom = send(value[middle:], along(targets, 2, 3))
    return value + jnp.concatenate([top, bottom], 0)


def one_near(value, targets):
    return value + send(value, along(targets, 1, 0)) + send(value, along(targets, 3, 0))


def one_y(value, targets):
    pairs = [(device(1 - y, x, c, b), device(y, x, c, b)) for b, (y, x, c) in targets.items()]
    return value + send(value, pairs)


CORE_SWAP = every(lambda y, x, c, h, z: (y, x, 1 - c, block(h, z)))
FROM_LEFT = every(lambda y, x, c, h, z: (y, x - 1, c, block(h, z)))
FROM_RIGHT = every(lambda y, x, c, h, z: (y, x + 1, c, block(h, z)))
FROM_UP = every(lambda y, x, c, h, z: (y, x, c, block(h, z + 1)))
FROM_DOWN = every(lambda y, x, c, h, z: (y, x, c, block(h, z - 1)))
FROM_OTHER = every(lambda y, x, c, h, z: (y, x, c, block(h + 1, z)))


def near(keep, got):
    middle = keep.shape[1] // 2
    far_top = send(keep[2, :middle] + got[2, :middle], FROM_LEFT)
    far_bottom = send(keep[2, middle:] + got[2, middle:], FROM_RIGHT)
    right = keep[1] + got[1]
    right = jnp.concatenate([right[:middle] + far_top, right[middle:]], 0)
    left = keep[3] + got[3]
    left = jnp.concatenate([left[:middle], left[middle:] + far_bottom], 0)
    return keep[0] + got[0], right, left


def together(*values):
    return lax.optimization_barrier(values)


def per_device(half_b):
    local, code_c, target_c, over, final = plan()
    aux, blk = lax.axis_index("aux"), lax.axis_index("blk")
    place = aux * GROUPS + blk
    table_a, table_b = jnp.asarray(local[0])[place], jnp.asarray(local[1])[place]
    table_c = jnp.asarray(code_c)[blk].reshape(1)

    held = {O: placed(half_b)}
    held[PZ] = send(half_b, FROM_UP)
    held[MZ] = send(half_b, FROM_DOWN)
    held[Y0] = send(half_b, FROM_OTHER)
    held[O], held[PZ], held[MZ], held[Y0] = together(held[O], held[PZ], held[MZ], held[Y0])

    held[PP] = send(held[PZ], FROM_UP)
    held[MM] = send(held[MZ], FROM_DOWN)
    held[Y1] = send(held[PZ], FROM_OTHER)
    keep, given = products(table_a, [held[n] for n in HELD_A], HELD_A, PAIRS_A, (NX, NX))
    own_a, right_a, left_a = near(keep, send(given, CORE_SWAP))
    total_a = own_a + send(right_a, FROM_LEFT) + send(left_a, FROM_RIGHT)
    total_a, held[PP], held[MM], held[Y1] = together(total_a, held[PP], held[MM], held[Y1])

    held[Y2] = send(held[PP], FROM_OTHER)
    keep, given = products(table_b, [held[n] for n in HELD_B], HELD_B, PAIRS_B, (NX, NX))
    own_b, right_b, left_b = near(keep, send(given, CORE_SWAP))
    own_b, right_b, left_b, held[Y2] = together(own_b, right_b, left_b, held[Y2])

    done_a = total_a + send(total_a, over[0])
    total_b = own_b + send(right_b, FROM_LEFT) + send(left_b, FROM_RIGHT)
    (part_c,) = products(table_c, [held[n] for n in HELD_C], HELD_C, PAIRS_C, (1,))
    part_c = one_far(one_core(part_c[0], target_c), target_c)
    done_a, total_b, part_c = together(done_a, total_b, part_c)

    top = send(done_a, final[0, 0])
    bottom = send(done_a, final[0, 1])
    done_b = total_b + send(total_b, over[1])
    done_c = one_y(one_near(part_c, target_c), target_c)
    top, bottom, done_b, done_c = together(top, bottom, done_b, done_c)

    top = top + send(done_b, final[1, 0]) + send(done_c, final[2, 0])
    bottom = bottom + send(done_b, final[1, 1]) + send(done_c, final[2, 1])
    return jnp.concatenate([top, bottom], 0)


def solution(mesh):
    placed = (P("aux", "blk", None),)
    return jax.shard_map(
        per_device, mesh=mesh, in_specs=placed, out_specs=P("blk", "aux"), check_vma=False
    )
```

```python
import collections
import functools
import random

import jax
import jax.numpy as jnp
import numpy as np
from jax import lax
from jax.experimental import pallas as pl
from jax.experimental.pallas import tpu as pltpu
from jax.sharding import PartitionSpec as P

ALL = ("aux", "blk")
NX, NZ, GROUPS = 4, 8, 16
VMEM_LIMIT = 16 * 2**20


def device(y_lo, x, core, blk):
    return ((y_lo * NX + x % NX) * 2 + core) * GROUPS + blk


def block(h, z):
    return h % 2 * NZ + z % NZ


def every(move):
    return [
        (device(*move(y_lo, x, core, h, z)), device(y_lo, x, core, block(h, z)))
        for y_lo in range(2)
        for x in range(NX)
        for core in range(2)
        for h in range(2)
        for z in range(NZ)
    ]


def send(value, pairs):
    return lax.ppermute(value, ALL, pairs)


O, PZ, MZ, Y0 = (0, 0), (0, 1), (0, -1), (1, 0)
PP, MM, Y1, Y2 = (0, 2), (0, -2), (1, 1), (1, 2)
HELD_A = (O, PZ, MZ, Y0)
HELD_B = (O, MZ, PP, MM, Y1)
HELD_C = (MM, Y2)


def units_of(pairs, h, z):
    found = []
    for at, (first, second, halves) in enumerate(pairs):
        i, j = block(h + first[0], z + first[1]), block(h + second[0], z + second[1])
        for half in halves(h, z):
            found.append(((at * 2 + (i > j)) * 2 + half, min(i, j), max(i, j), half))
    return found


def both(h, z):
    return (0, 1)


def by_h(h, z):
    return (h,)


def by_z(h, z):
    return (0,) if 2 <= z < 6 else (1,)


def upper(h, z):
    return (0,)


def lower(h, z):
    return (1,)


PAIRS_A = ((O, PZ, both), (MZ, PZ, both), (O, Y0, by_h), (MZ, Y0, both), (O, O, upper))
PAIRS_B = ((MZ, PP, both), (MM, PP, by_z), (MZ, Y1, both), (MM, Y1, both), (O, O, lower))
PAIRS_C = ((MM, Y2, by_h),)


def steps(a, b, n):
    ahead, back = (b - a) % n, (a - b) % n
    share = 0.5 if ahead == back else 1.0
    found = []
    if ahead and ahead <= back:
        found += [((a + i) % n, 1, share) for i in range(ahead)]
    if ahead and back <= ahead:
        found += [((a - i) % n, -1, share) for i in range(back)]
    return found


@functools.cache
def route(source, target):
    found = []
    for order in ((0, 1, 2), (2, 1, 0)):
        at = list(source)
        for axis in order:
            for place, way, share in steps(at[axis], target[axis], (NX, 4, NZ)[axis]):
                link = at[:axis] + [place] + at[axis + 1 :]
                found.append(((order, axis, way, *link), share))
            at[axis] = target[axis]
    return found


def links(own, place, y, row, col):
    h, z = own // NZ, own % NZ
    x = place // 2
    return route((x, 2 * h + y, z), (col // 2 % NX, row // NZ * 2 + col // NZ, row % NZ)) + [((own, x, y), 1.0)]


@functools.cache
def spread(pairs, trials=20000):
    draw = random.Random(0)
    units = [units_of(pairs, own // NZ, own % NZ) for own in range(GROUPS)]
    places = [list(range(8)) for _ in range(GROUPS)]
    planes = [
        [own // NZ if row // NZ == col // NZ else 1 - own // NZ for _, row, col, _ in units[own]]
        for own in range(GROUPS)
    ]
    load = collections.Counter()
    for own in range(GROUPS):
        for (_, row, col, _), place, y in zip(units[own], places[own], planes[own]):
            for link, share in links(own, place, y, row, col):
                load[link] += share
    for _ in range(trials):
        own, u, v = draw.randrange(GROUPS), draw.randrange(8), draw.randrange(8)
        place, y = places[own], planes[own]
        moved = [(u, place[v], y[u]), (v, place[u], y[v])] if u != v else [(u, place[u], 1 - y[u])]
        change = collections.Counter()
        for w, new_place, new_y in moved:
            _, row, col, _ = units[own][w]
            for link, share in links(own, place[w], y[w], row, col):
                change[link] -= share
            for link, share in links(own, new_place, new_y, row, col):
                change[link] += share
        if sum((load[k] + d) ** 4 - load[k] ** 4 for k, d in change.items()) <= 0:
            load.update(change)
            for w, new_place, new_y in moved:
                place[w], y[w] = new_place, new_y
    return [list(zip(units[own], places[own], planes[own])) for own in range(GROUPS)]


@functools.cache
def plan():
    tables = np.zeros((2, GROUPS, 2, NX), np.int32)
    code_c = np.zeros((GROUPS,), np.int32)
    target_c = {}
    over = {0: [], 1: []}
    final = {(batch, half): [] for batch in (0, 1) for half in (0, 1)}
    final_c = {(y, half): [] for y in (0, 1) for half in (0, 1)}
    for h in range(2):
        for z in range(NZ):
            own = block(h, z)
            for batch in range(2):
                for (code, row, col, half), place, y in spread(PAIRS_B if batch else PAIRS_A)[own]:
                    x, core = place // 2, place % 2
                    tables[batch, own, core, x] = code
                    over[batch].append((device(1 - y, x, core, own), device(y, x, core, own)))
                    final[batch, half].append((device(y, x, core, own), col * GROUPS + row))
            ((code, row, col, half),) = units_of(PAIRS_C, h, z)
            code_c[own] = code
            target_c[own] = (1 - h, col // 2 % NX, col % 2)
            for y in (0, 1):
                final_c[y, half].append((device(y, *target_c[own][1:], own), col * GROUPS + row))
    local = np.zeros((2, 16, GROUPS, 2, NX), np.int32)
    for aux in range(16):
        x, core = aux // 2 % NX, aux % 2
        for j in range(NX):
            local[:, aux, :, 0, j] = tables[:, :, core, (x + j) % NX]
            local[:, aux, :, 1, j] = tables[:, :, 1 - core, (x + j) % NX]
    return local.reshape(2, 16 * GROUPS, 2 * NX), code_c, target_c, over, final, final_c


def dot_t(a, b):
    return lax.dot_general(a, b, (((1,), (1,)), ((), ())), preferred_element_type=jnp.float32)


def half_product(rows, cols, half):
    at = pl.ds(pl.multiple_of(half * 256, 256), 256)
    total = dot_t(rows[0, at, :], cols[0])
    for k in range(1, rows.shape[0]):
        total += dot_t(rows[k, at, :], cols[k])
    return total


def units_kernel(index_pairs, spare, table, *refs):
    held, outs = refs[: len(refs) - spare], refs[len(refs) - spare :]

    def slot(base, out, j, carry):
        code = table[base + j]
        half = code % 2
        for at, (first, second) in enumerate(index_pairs):

            @pl.when(code // 2 == at * 2)
            def _():
                out[j] = half_product(held[first], held[second], half)

            if first != second:

                @pl.when(code // 2 == at * 2 + 1)
                def _():
                    out[j] = half_product(held[second], held[first], half)

        return carry

    base = 0
    for out in outs:
        lax.fori_loop(0, out.shape[0], functools.partial(slot, base, out), 0)
        base += out.shape[0]


def products(table, held, names, pairs, counts):
    index_pairs = tuple((names.index(a), names.index(b)) for a, b, _ in pairs)
    return pl.pallas_call(
        functools.partial(units_kernel, index_pairs, len(counts)),
        out_shape=[pltpu.VMEM((count, 256, 512), jnp.float32) for count in counts],
        in_specs=[pl.BlockSpec(memory_space=pltpu.SMEM)]
        + [pl.BlockSpec(memory_space=pltpu.VMEM)] * len(held),
        out_specs=[pl.BlockSpec(memory_space=pltpu.VMEM)] * len(counts),
        compiler_params=pltpu.CompilerParams(vmem_limit_bytes=VMEM_LIMIT),
    )(table, *held)


def toward(targets, source, only):
    return [
        (device(*source(y, x, c, step), b), device(*only(y, x, c, step), b))
        for b, (y, x, c) in targets.items()
        for step in range(8)
    ]


def copy_kernel(source, out):
    out[...] = source[...]


def placed(value):
    return pl.pallas_call(
        copy_kernel,
        out_shape=pltpu.VMEM(value.shape, value.dtype),
        in_specs=[pl.BlockSpec(memory_space=pltpu.VMEM)],
        out_specs=pl.BlockSpec(memory_space=pltpu.VMEM),
        compiler_params=pltpu.CompilerParams(vmem_limit_bytes=VMEM_LIMIT),
    )(value)


def one_core(value, targets):
    def at(core_of):
        return lambda y, x, c, step: (step // NX, x + step % NX, core_of(c))

    return value + send(value, toward(targets, at(lambda c: 1 - c), at(lambda c: c)))


def along(targets, offset_from, offset_to):
    def at(offset):
        return lambda y, x, c, step: (step % 2, x + offset, c)

    return sorted(set(toward(targets, at(offset_from), at(offset_to))))


def one_far(value, targets):
    middle = value.shape[0] // 2
    top = send(value[:middle], along(targets, 2, 1))
    bottom = send(value[middle:], along(targets, 2, 3))
    return value + jnp.concatenate([top, bottom], 0)


def one_near(value, targets):
    return value + send(value, along(targets, 1, 0)) + send(value, along(targets, 3, 0))


CORE_SWAP = every(lambda y, x, c, h, z: (y, x, 1 - c, block(h, z)))
FROM_LEFT = every(lambda y, x, c, h, z: (y, x - 1, c, block(h, z)))
FROM_RIGHT = every(lambda y, x, c, h, z: (y, x + 1, c, block(h, z)))
FROM_UP = every(lambda y, x, c, h, z: (y, x, c, block(h, z + 1)))
FROM_DOWN = every(lambda y, x, c, h, z: (y, x, c, block(h, z - 1)))
FROM_OTHER = every(lambda y, x, c, h, z: (y, x, c, block(h + 1, z)))


def near(keep, got):
    middle = keep.shape[1] // 2
    far_top = send(keep[2, :middle] + got[2, :middle], FROM_LEFT)
    far_bottom = send(keep[2, middle:] + got[2, middle:], FROM_RIGHT)
    right = keep[1] + got[1]
    right = jnp.concatenate([right[:middle] + far_top, right[middle:]], 0)
    left = keep[3] + got[3]
    left = jnp.concatenate([left[:middle], left[middle:] + far_bottom], 0)
    return keep[0] + got[0], right, left


def together(*values):
    return lax.optimization_barrier(values)


def per_device(half_b):
    local, code_c, target_c, over, final, final_c = plan()
    aux, blk = lax.axis_index("aux"), lax.axis_index("blk")
    place = aux * GROUPS + blk
    table_a, table_b = jnp.asarray(local[0])[place], jnp.asarray(local[1])[place]
    table_c = jnp.asarray(code_c)[blk].reshape(1)

    held = {O: placed(half_b)}
    held[PZ] = send(half_b, FROM_UP)
    held[MZ] = send(half_b, FROM_DOWN)
    held[Y0] = send(half_b, FROM_OTHER)
    held[O], held[PZ], held[MZ], held[Y0] = together(held[O], held[PZ], held[MZ], held[Y0])

    held[PP] = send(held[PZ], FROM_UP)
    held[MM] = send(held[MZ], FROM_DOWN)
    held[Y1] = send(held[PZ], FROM_OTHER)
    keep, given = products(table_a, [held[n] for n in HELD_A], HELD_A, PAIRS_A, (NX, NX))
    own_a, right_a, left_a = near(keep, send(given, CORE_SWAP))
    total_a = own_a + send(right_a, FROM_LEFT) + send(left_a, FROM_RIGHT)
    total_a, held[PP], held[MM], held[Y1] = together(total_a, held[PP], held[MM], held[Y1])

    held[Y2] = send(held[PP], FROM_OTHER)
    keep, given = products(table_b, [held[n] for n in HELD_B], HELD_B, PAIRS_B, (NX, NX))
    own_b, right_b, left_b = near(keep, send(given, CORE_SWAP))
    own_b, right_b, left_b = together(own_b, right_b, left_b)

    done_a = total_a + send(total_a, over[0])
    total_b = own_b + send(right_b, FROM_LEFT) + send(left_b, FROM_RIGHT)
    done_a, total_b, held[Y2] = together(done_a, total_b, held[Y2])

    top = send(done_a, final[0, 0])
    bottom = send(done_a, final[0, 1])
    done_b = total_b + send(total_b, over[1])
    (part_c,) = products(table_c, [held[n] for n in HELD_C], HELD_C, PAIRS_C, (1,))
    part_c = one_far(one_core(part_c[0], target_c), target_c)
    top, bottom, part_c = together(top, bottom, part_c)
    part_c = one_near(part_c, target_c)
    top, bottom, done_b, part_c = together(top, bottom, done_b, part_c)

    top = top + send(done_b, final[1, 0]) + send(part_c, final_c[0, 0]) + send(part_c, final_c[1, 0])
    bottom = bottom + send(done_b, final[1, 1]) + send(part_c, final_c[0, 1]) + send(part_c, final_c[1, 1])
    return jnp.concatenate([top, bottom], 0)


def solution(mesh):
    placed = (P("aux", "blk", None),)
    return jax.shard_map(
        per_device, mesh=mesh, in_specs=placed, out_specs=P("blk", "aux"), check_vma=False
    )
```

```python
import collections
import functools
import random

import jax
import jax.numpy as jnp
import numpy as np
from jax import lax
from jax.experimental import pallas as pl
from jax.experimental.pallas import tpu as pltpu
from jax.sharding import PartitionSpec as P

ALL = ("aux", "blk")
NX, NZ, GROUPS = 4, 8, 16
VMEM_LIMIT = 16 * 2**20


def device(y_lo, x, core, blk):
    return ((y_lo * NX + x % NX) * 2 + core) * GROUPS + blk


def block(h, z):
    return h % 2 * NZ + z % NZ


def every(move):
    return [
        (device(*move(y_lo, x, core, h, z)), device(y_lo, x, core, block(h, z)))
        for y_lo in range(2)
        for x in range(NX)
        for core in range(2)
        for h in range(2)
        for z in range(NZ)
    ]


def send(value, pairs):
    return lax.ppermute(value, ALL, pairs)


O, PZ, MZ, Y0 = (0, 0), (0, 1), (0, -1), (1, 0)
PP, MM, Y1, Y2 = (0, 2), (0, -2), (1, 1), (1, 2)
HELD_A = (O, PZ, MZ, Y0)
HELD_B = (O, MZ, PP, MM, Y1)
HELD_C = (MM, Y2)


def units_of(pairs, h, z):
    found = []
    for at, (first, second, halves) in enumerate(pairs):
        i, j = block(h + first[0], z + first[1]), block(h + second[0], z + second[1])
        for half in halves(h, z):
            found.append(((at * 2 + (i > j)) * 2 + half, min(i, j), max(i, j), half))
    return found


def both(h, z):
    return (0, 1)


def by_h(h, z):
    return (h,)


def by_z(h, z):
    return (0,) if 2 <= z < 6 else (1,)


def upper(h, z):
    return (0,)


def lower(h, z):
    return (1,)


PAIRS_A = ((O, PZ, both), (MZ, PZ, both), (O, Y0, by_h), (MZ, Y0, both), (O, O, upper))
PAIRS_B = ((MZ, PP, both), (MM, PP, by_z), (MZ, Y1, both), (MM, Y1, both), (O, O, lower))
PAIRS_C = ((MM, Y2, by_h),)


def steps(a, b, n):
    ahead, back = (b - a) % n, (a - b) % n
    share = 0.5 if ahead == back else 1.0
    found = []
    if ahead and ahead <= back:
        found += [((a + i) % n, 1, share) for i in range(ahead)]
    if ahead and back <= ahead:
        found += [((a - i) % n, -1, share) for i in range(back)]
    return found


@functools.cache
def route(source, target):
    found = []
    for weight, order in ((0.05, (0, 1, 2)), (1.0, (2, 1, 0))):
        at = list(source)
        for axis in order:
            for place, way, share in steps(at[axis], target[axis], (NX, 4, NZ)[axis]):
                link = at[:axis] + [place] + at[axis + 1 :]
                found.append(((weight, axis, way, *link), share))
            at[axis] = target[axis]
    return found


def links(own, place, y, unit):
    h, z = own // NZ, own % NZ
    _, row, col, _ = unit
    return route((place // 2, 2 * h + y, z), (col // 2 % NX, row // NZ * 2 + col // NZ, row % NZ))


@functools.cache
def spread(trials=40000):
    draw = random.Random(0)
    where = [(own // NZ, own % NZ) for own in range(GROUPS)]
    units = [[units_of(pairs, h, z) for pairs in (PAIRS_A, PAIRS_B)] for h, z in where]
    at = [[list(range(8)), list(range(8))] for _ in where]
    planes = [[h] * 8 for h, _ in where]
    load = collections.Counter()

    def on(own, batch, place, index, y):
        return links(own, place, 1 - y if batch else y, units[own][batch][index])

    for own, (h, z) in enumerate(where):
        for batch in (0, 1):
            for place in range(8):
                for link, share in on(own, batch, place, at[own][batch][place], planes[own][place]):
                    load[link] += share
        for unit in units_of(PAIRS_C, h, z):
            for y in (0, 1):
                for link, share in links(own, unit[2] % 8, y, unit):
                    load[link] += share
    for _ in range(trials):
        own, batch, u, v = draw.randrange(GROUPS), draw.randrange(2), draw.randrange(8), draw.randrange(8)
        now, plane = at[own], planes[own]
        change = collections.Counter()
        if u == v:
            for one in (0, 1):
                for sign, y in ((-1, plane[u]), (1, 1 - plane[u])):
                    for link, share in on(own, one, u, now[one][u], y):
                        change[link] += sign * share
        else:
            i, j = now[batch][u], now[batch][v]
            for sign, place, index in ((-1, u, i), (-1, v, j), (1, u, j), (1, v, i)):
                for link, share in on(own, batch, place, index, plane[place]):
                    change[link] += sign * share
        if sum(link[0] * ((load[link] + d) ** 4 - load[link] ** 4) for link, d in change.items()) <= 0:
            for link, d in change.items():
                load[link] += d
            if u == v:
                plane[u] = 1 - plane[u]
            else:
                now[batch][u], now[batch][v] = j, i
    return units, at, planes


@functools.cache
def plan():
    tables = np.zeros((2, GROUPS, 2, NX), np.int32)
    code_c = np.zeros((GROUPS,), np.int32)
    target_c = {}
    final = {half: [] for half in (0, 1)}
    final_c = {(y, half): [] for y in (0, 1) for half in (0, 1)}
    first = np.zeros((16, GROUPS), np.bool_)
    units, at, planes = spread()
    for h in range(2):
        for z in range(NZ):
            own = block(h, z)
            for place in range(8):
                x, core = place // 2, place % 2
                for batch in range(2):
                    code, row, col, half = units[own][batch][at[own][batch][place]]
                    y = 1 - planes[own][place] if batch else planes[own][place]
                    tables[batch, own, core, x] = code
                    final[half].append((device(y, x, core, own), col * GROUPS + row))
                    first[(y * NX + x) * 2 + core, own] = not batch
            ((code, row, col, half),) = units_of(PAIRS_C, h, z)
            code_c[own] = code
            target_c[own] = (1 - h, col // 2 % NX, col % 2)
            for y in (0, 1):
                final_c[y, half].append((device(y, *target_c[own][1:], own), col * GROUPS + row))
    local = np.zeros((2, 16, GROUPS, 2, NX), np.int32)
    for aux in range(16):
        x, core = aux // 2 % NX, aux % 2
        for j in range(NX):
            local[:, aux, :, 0, j] = tables[:, :, core, (x + j) % NX]
            local[:, aux, :, 1, j] = tables[:, :, 1 - core, (x + j) % NX]
    return local.reshape(2, 16 * GROUPS, 2 * NX), code_c, target_c, first, final, final_c


def dot_t(a, b):
    return lax.dot_general(a, b, (((1,), (1,)), ((), ())), preferred_element_type=jnp.float32)


def half_product(rows, cols, half):
    at = pl.ds(pl.multiple_of(half * 256, 256), 256)
    total = dot_t(rows[0, at, :], cols[0])
    for k in range(1, rows.shape[0]):
        total += dot_t(rows[k, at, :], cols[k])
    return total


def units_kernel(index_pairs, spare, table, *refs):
    held, outs = refs[: len(refs) - spare], refs[len(refs) - spare :]

    def slot(base, out, j, carry):
        code = table[base + j]
        half = code % 2
        for at, (first, second) in enumerate(index_pairs):

            @pl.when(code // 2 == at * 2)
            def _():
                out[j] = half_product(held[first], held[second], half)

            if first != second:

                @pl.when(code // 2 == at * 2 + 1)
                def _():
                    out[j] = half_product(held[second], held[first], half)

        return carry

    base = 0
    for out in outs:
        lax.fori_loop(0, out.shape[0], functools.partial(slot, base, out), 0)
        base += out.shape[0]


def products(table, held, names, pairs, counts):
    index_pairs = tuple((names.index(a), names.index(b)) for a, b, _ in pairs)
    return pl.pallas_call(
        functools.partial(units_kernel, index_pairs, len(counts)),
        out_shape=[pltpu.VMEM((count, 256, 512), jnp.float32) for count in counts],
        in_specs=[pl.BlockSpec(memory_space=pltpu.SMEM)]
        + [pl.BlockSpec(memory_space=pltpu.VMEM)] * len(held),
        out_specs=[pl.BlockSpec(memory_space=pltpu.VMEM)] * len(counts),
        compiler_params=pltpu.CompilerParams(vmem_limit_bytes=VMEM_LIMIT),
    )(table, *held)


def toward(targets, source, only):
    return [
        (device(*source(y, x, c, step), b), device(*only(y, x, c, step), b))
        for b, (y, x, c) in targets.items()
        for step in range(8)
    ]


def copy_kernel(source, out):
    out[...] = source[...]


def placed(value):
    return pl.pallas_call(
        copy_kernel,
        out_shape=pltpu.VMEM(value.shape, value.dtype),
        in_specs=[pl.BlockSpec(memory_space=pltpu.VMEM)],
        out_specs=pl.BlockSpec(memory_space=pltpu.VMEM),
        compiler_params=pltpu.CompilerParams(vmem_limit_bytes=VMEM_LIMIT),
    )(value)


def one_core(value, targets):
    def at(core_of):
        return lambda y, x, c, step: (step // NX, x + step % NX, core_of(c))

    return value + send(value, toward(targets, at(lambda c: 1 - c), at(lambda c: c)))


def along(targets, offset_from, offset_to):
    def at(offset):
        return lambda y, x, c, step: (step % 2, x + offset, c)

    return sorted(set(toward(targets, at(offset_from), at(offset_to))))


def one_far(value, targets):
    middle = value.shape[0] // 2
    top = send(value[:middle], along(targets, 2, 1))
    bottom = send(value[middle:], along(targets, 2, 3))
    return value + jnp.concatenate([top, bottom], 0)


def one_near(value, targets):
    return value + send(value, along(targets, 1, 0)) + send(value, along(targets, 3, 0))


Y_SWAP = every(lambda y, x, c, h, z: (1 - y, x, c, block(h, z)))
CORE_SWAP = every(lambda y, x, c, h, z: (y, x, 1 - c, block(h, z)))
FROM_LEFT = every(lambda y, x, c, h, z: (y, x - 1, c, block(h, z)))
FROM_RIGHT = every(lambda y, x, c, h, z: (y, x + 1, c, block(h, z)))
FROM_UP = every(lambda y, x, c, h, z: (y, x, c, block(h, z + 1)))
FROM_DOWN = every(lambda y, x, c, h, z: (y, x, c, block(h, z - 1)))
FROM_OTHER = every(lambda y, x, c, h, z: (y, x, c, block(h + 1, z)))


def near(keep, got):
    middle = keep.shape[1] // 2
    far_top = send(keep[2, :middle] + got[2, :middle], FROM_LEFT)
    far_bottom = send(keep[2, middle:] + got[2, middle:], FROM_RIGHT)
    right = keep[1] + got[1]
    right = jnp.concatenate([right[:middle] + far_top, right[middle:]], 0)
    left = keep[3] + got[3]
    left = jnp.concatenate([left[:middle], left[middle:] + far_bottom], 0)
    return keep[0] + got[0], right, left


def together(*values):
    return lax.optimization_barrier(values)


def per_device(half_b):
    local, code_c, target_c, first, final, final_c = plan()
    aux, blk = lax.axis_index("aux"), lax.axis_index("blk")
    place = aux * GROUPS + blk
    table_a, table_b = jnp.asarray(local[0])[place], jnp.asarray(local[1])[place]
    table_c = jnp.asarray(code_c)[blk].reshape(1)

    held = {O: placed(half_b)}
    held[PZ] = send(half_b, FROM_UP)
    held[MZ] = send(half_b, FROM_DOWN)
    held[Y0] = send(half_b, FROM_OTHER)
    held[O], held[PZ], held[MZ], held[Y0] = together(held[O], held[PZ], held[MZ], held[Y0])

    held[PP] = send(held[PZ], FROM_UP)
    held[MM] = send(held[MZ], FROM_DOWN)
    held[Y1] = send(held[PZ], FROM_OTHER)
    keep, given = products(table_a, [held[n] for n in HELD_A], HELD_A, PAIRS_A, (NX, NX))
    own_a, right_a, left_a = near(keep, send(given, CORE_SWAP))
    total_a = own_a + send(right_a, FROM_LEFT) + send(left_a, FROM_RIGHT)
    total_a, held[PP], held[MM], held[Y1] = together(total_a, held[PP], held[MM], held[Y1])

    held[Y2] = send(held[PP], FROM_OTHER)
    keep, given = products(table_b, [held[n] for n in HELD_B], HELD_B, PAIRS_B, (NX, NX))
    own_b, right_b, left_b = near(keep, send(given, CORE_SWAP))
    own_b, right_b, left_b = together(own_b, right_b, left_b)

    total_b = own_b + send(right_b, FROM_LEFT) + send(left_b, FROM_RIGHT)
    total_b, held[Y2] = together(total_b, held[Y2])

    has_first = jnp.asarray(first)[aux, blk]
    done = jnp.where(has_first, total_a, total_b) + send(jnp.where(has_first, total_b, total_a), Y_SWAP)
    (part_c,) = products(table_c, [held[n] for n in HELD_C], HELD_C, PAIRS_C, (1,))
    part_c = one_near(one_far(one_core(part_c[0], target_c), target_c), target_c)
    done, part_c = together(done, part_c)

    top = send(done, final[0]) + send(part_c, final_c[0, 0]) + send(part_c, final_c[1, 0])
    bottom = send(done, final[1]) + send(part_c, final_c[0, 1]) + send(part_c, final_c[1, 1])
    return jnp.concatenate([top, bottom], 0)


def solution(mesh):
    placed = (P("aux", "blk", None),)
    return jax.shard_map(
        per_device, mesh=mesh, in_specs=placed, out_specs=P("blk", "aux"), check_vma=False
    )
```

```python
import collections
import functools
import random

import jax
import jax.numpy as jnp
import numpy as np
from jax import lax
from jax.experimental import pallas as pl
from jax.experimental.pallas import tpu as pltpu
from jax.sharding import PartitionSpec as P

ALL = ("aux", "blk")
NX, NZ, GROUPS = 4, 8, 16
VMEM_LIMIT = 16 * 2**20


def device(y_lo, x, core, blk):
    return ((y_lo * NX + x % NX) * 2 + core) * GROUPS + blk


def block(h, z):
    return h % 2 * NZ + z % NZ


def every(move):
    return [
        (device(*move(y_lo, x, core, h, z)), device(y_lo, x, core, block(h, z)))
        for y_lo in range(2)
        for x in range(NX)
        for core in range(2)
        for h in range(2)
        for z in range(NZ)
    ]


def send(value, pairs):
    return lax.ppermute(value, ALL, pairs)


O, PZ, MZ, Y0 = (0, 0), (0, 1), (0, -1), (1, 0)
PP, MM, Y1, Y2 = (0, 2), (0, -2), (1, 1), (1, 2)
HELD_A = (O, PZ, MZ, Y0)
HELD_B = (O, MZ, PP, MM, Y1)
HELD_C = (MM, Y2)


def units_of(pairs, h, z):
    found = []
    for at, (first, second, halves) in enumerate(pairs):
        i, j = block(h + first[0], z + first[1]), block(h + second[0], z + second[1])
        for half in halves(h, z):
            core = half if halves is both else int(first == second)
            found.append(((at, int(i > j), core), min(i, j), max(i, j), half))
    return found


def both(h, z):
    return (0, 1)


def by_h(h, z):
    return (h,)


def by_z(h, z):
    return (0,) if 2 <= z < 6 else (1,)


def upper(h, z):
    return (0,)


def lower(h, z):
    return (1,)


PAIRS_A = ((O, PZ, both), (MZ, PZ, both), (O, Y0, by_h), (MZ, Y0, both), (O, O, upper))
PAIRS_B = ((MZ, PP, both), (MM, PP, by_z), (MZ, Y1, both), (MM, Y1, both), (O, O, lower))
PAIRS_C = ((MM, Y2, by_h),)


def steps(a, b, n):
    ahead, back = (b - a) % n, (a - b) % n
    share = 0.5 if ahead == back else 1.0
    found = []
    if ahead and ahead <= back:
        found += [((a + i) % n, 1, share) for i in range(ahead)]
    if ahead and back <= ahead:
        found += [((a - i) % n, -1, share) for i in range(back)]
    return found


@functools.cache
def route(source, target):
    found = []
    for weight, order in ((0.05, (0, 1, 2)), (1.0, (2, 1, 0))):
        at = list(source)
        for axis in order:
            for place, way, share in steps(at[axis], target[axis], (NX, 4, NZ)[axis]):
                link = at[:axis] + [place] + at[axis + 1 :]
                found.append(((weight, axis, way, *link), share))
            at[axis] = target[axis]
    return found


def links(own, place, y, unit):
    h, z = own // NZ, own % NZ
    _, row, col, _ = unit
    return route((place // 2, 2 * h + y, z), (col // 2 % NX, row // NZ * 2 + col // NZ, row % NZ))


def by_core(units):
    cores = [[index for index, unit in enumerate(units) if unit[0][2] == core] for core in (0, 1)]
    return [cores[place % 2][place // 2] for place in range(8)]


@functools.cache
def spread(trials=40000):
    draw = random.Random(0)
    where = [(own // NZ, own % NZ) for own in range(GROUPS)]
    units = [[units_of(pairs, h, z) for pairs in (PAIRS_A, PAIRS_B)] for h, z in where]
    at = [[by_core(batch) for batch in both_batches] for both_batches in units]
    planes = [[h] * 8 for h, _ in where]
    load = collections.Counter()

    def on(own, batch, place, index, y):
        return links(own, place, 1 - y if batch else y, units[own][batch][index])

    for own, (h, z) in enumerate(where):
        for batch in (0, 1):
            for place in range(8):
                for link, share in on(own, batch, place, at[own][batch][place], planes[own][place]):
                    load[link] += share
        for unit in units_of(PAIRS_C, h, z):
            for y in (0, 1):
                for link, share in links(own, unit[2] % 8, y, unit):
                    load[link] += share
    for _ in range(trials):
        own, batch, u, v = draw.randrange(GROUPS), draw.randrange(2), draw.randrange(8), draw.randrange(8)
        if (u - v) % 2:
            continue
        now, plane = at[own], planes[own]
        change = collections.Counter()
        if u == v:
            for one in (0, 1):
                for sign, y in ((-1, plane[u]), (1, 1 - plane[u])):
                    for link, share in on(own, one, u, now[one][u], y):
                        change[link] += sign * share
        else:
            i, j = now[batch][u], now[batch][v]
            for sign, place, index in ((-1, u, i), (-1, v, j), (1, u, j), (1, v, i)):
                for link, share in on(own, batch, place, index, plane[place]):
                    change[link] += sign * share
        if sum(link[0] * ((load[link] + d) ** 4 - load[link] ** 4) for link, d in change.items()) <= 0:
            for link, d in change.items():
                load[link] += d
            if u == v:
                plane[u] = 1 - plane[u]
            else:
                now[batch][u], now[batch][v] = j, i
    return units, at, planes


@functools.cache
def plan():
    tables = np.zeros((2, 16, GROUPS, 5, 4), np.int32)
    table_c = np.zeros((GROUPS, 4), np.int32)
    target_c = {}
    final = {half: [] for half in (0, 1)}
    final_c = {(y, half): [] for y in (0, 1) for half in (0, 1)}
    first = np.zeros((16, GROUPS), np.bool_)
    units, at, planes = spread()
    for h in range(2):
        for z in range(NZ):
            own = block(h, z)
            for place in range(8):
                x, core = place // 2, place % 2
                for batch in range(2):
                    (pair, swap, _), row, col, half = units[own][batch][at[own][batch][place]]
                    y = 1 - planes[own][place] if batch else planes[own][place]
                    final[half].append((device(y, x, core, own), col * GROUPS + row))
                    first[(y * NX + x) * 2 + core, own] = not batch
                    for aux in range(16):
                        entry, offset = tables[batch, aux, own, pair], (x - aux // 2) % NX
                        kept = aux % 2 == core
                        entry[0] = swap
                        if (PAIRS_A, PAIRS_B)[batch][pair][2] is both:
                            entry[1 if kept else 2] = offset
                            entry[3] = aux % 2
                        else:
                            entry[1:] = offset, kept, half
            (((_, swap, _), row, col, half),) = units_of(PAIRS_C, h, z)
            table_c[own] = swap, 0, 1, half
            target_c[own] = (1 - h, col // 2 % NX, col % 2)
            for y in (0, 1):
                final_c[y, half].append((device(y, *target_c[own][1:], own), col * GROUPS + row))
    return tables.reshape(2, 16 * GROUPS, 20), table_c, target_c, first, final, final_c


def dot_t(a, b):
    return lax.dot_general(a, b, (((1,), (1,)), ((), ())), preferred_element_type=jnp.float32)


def half_product(rows, cols, half):
    at = pl.ds(pl.multiple_of(half * 256, 256), 256)
    total = dot_t(rows[0, at, :], cols[0])
    for k in range(1, rows.shape[0]):
        total += dot_t(rows[k, at, :], cols[k])
    return total


def units_kernel(pairs, index_pairs, spare, table, *refs):
    held, outs = refs[: len(refs) - spare], refs[len(refs) - spare :]
    for at, ((first, second), (_, _, halves)) in enumerate(zip(index_pairs, pairs)):
        swap, one, two, half = (table[4 * at + i] for i in range(4))
        for turned in range(1 if first == second else 2):
            rows, cols = (held[second], held[first]) if turned else (held[first], held[second])
            if halves is both:

                @pl.when(swap == turned)
                def _():
                    outs[1][two] = half_product(rows, cols, 1 - half)
                    outs[0][one] = half_product(rows, cols, half)

            else:
                for mine in range(2 - len(outs), 2):

                    @pl.when((swap == turned) & (two == mine))
                    def _():
                        outs[1 - mine][one] = half_product(rows, cols, half)


def products(table, held, names, pairs, counts):
    index_pairs = tuple((names.index(a), names.index(b)) for a, b, _ in pairs)
    return pl.pallas_call(
        functools.partial(units_kernel, pairs, index_pairs, len(counts)),
        out_shape=[pltpu.VMEM((count, 256, 512), jnp.float32) for count in counts],
        in_specs=[pl.BlockSpec(memory_space=pltpu.SMEM)]
        + [pl.BlockSpec(memory_space=pltpu.VMEM)] * len(held),
        out_specs=[pl.BlockSpec(memory_space=pltpu.VMEM)] * len(counts),
        compiler_params=pltpu.CompilerParams(vmem_limit_bytes=VMEM_LIMIT),
    )(table, *held)


def toward(targets, source, only):
    return [
        (device(*source(y, x, c, step), b), device(*only(y, x, c, step), b))
        for b, (y, x, c) in targets.items()
        for step in range(8)
    ]


def copy_kernel(source, out):
    out[...] = source[...]


def placed(value):
    return pl.pallas_call(
        copy_kernel,
        out_shape=pltpu.VMEM(value.shape, value.dtype),
        in_specs=[pl.BlockSpec(memory_space=pltpu.VMEM)],
        out_specs=pl.BlockSpec(memory_space=pltpu.VMEM),
        compiler_params=pltpu.CompilerParams(vmem_limit_bytes=VMEM_LIMIT),
    )(value)


def one_core(value, targets):
    def at(core_of):
        return lambda y, x, c, step: (step // NX, x + step % NX, core_of(c))

    return value + send(value, toward(targets, at(lambda c: 1 - c), at(lambda c: c)))


def along(targets, offset_from, offset_to):
    def at(offset):
        return lambda y, x, c, step: (step % 2, x + offset, c)

    return sorted(set(toward(targets, at(offset_from), at(offset_to))))


def one_far(value, targets):
    middle = value.shape[0] // 2
    top = send(value[:middle], along(targets, 2, 1))
    bottom = send(value[middle:], along(targets, 2, 3))
    return value + jnp.concatenate([top, bottom], 0)


def one_near(value, targets):
    return value + send(value, along(targets, 1, 0)) + send(value, along(targets, 3, 0))


Y_SWAP = every(lambda y, x, c, h, z: (1 - y, x, c, block(h, z)))
CORE_SWAP = every(lambda y, x, c, h, z: (y, x, 1 - c, block(h, z)))
FROM_LEFT = every(lambda y, x, c, h, z: (y, x - 1, c, block(h, z)))
FROM_RIGHT = every(lambda y, x, c, h, z: (y, x + 1, c, block(h, z)))
FROM_UP = every(lambda y, x, c, h, z: (y, x, c, block(h, z + 1)))
FROM_DOWN = every(lambda y, x, c, h, z: (y, x, c, block(h, z - 1)))
FROM_OTHER = every(lambda y, x, c, h, z: (y, x, c, block(h + 1, z)))


def near(keep, got):
    middle = keep.shape[1] // 2
    far_top = send(keep[2, :middle] + got[2, :middle], FROM_LEFT)
    far_bottom = send(keep[2, middle:] + got[2, middle:], FROM_RIGHT)
    right = keep[1] + got[1]
    right = jnp.concatenate([right[:middle] + far_top, right[middle:]], 0)
    left = keep[3] + got[3]
    left = jnp.concatenate([left[:middle], left[middle:] + far_bottom], 0)
    return keep[0] + got[0], right, left


def together(*values):
    return lax.optimization_barrier(values)


def per_device(half_b):
    local, codes_c, target_c, first, final, final_c = plan()
    aux, blk = lax.axis_index("aux"), lax.axis_index("blk")
    place = aux * GROUPS + blk
    table_a, table_b = jnp.asarray(local[0])[place], jnp.asarray(local[1])[place]
    table_c = jnp.asarray(codes_c)[blk]

    held = {O: placed(half_b)}
    held[PZ] = send(half_b, FROM_UP)
    held[MZ] = send(half_b, FROM_DOWN)
    held[Y0] = send(half_b, FROM_OTHER)
    held[O], held[PZ], held[MZ], held[Y0] = together(held[O], held[PZ], held[MZ], held[Y0])

    held[PP] = send(held[PZ], FROM_UP)
    held[MM] = send(held[MZ], FROM_DOWN)
    held[Y1] = send(held[PZ], FROM_OTHER)
    keep, given = products(table_a, [held[n] for n in HELD_A], HELD_A, PAIRS_A, (NX, NX))
    own_a, right_a, left_a = near(keep, send(given, CORE_SWAP))
    total_a = own_a + send(right_a, FROM_LEFT) + send(left_a, FROM_RIGHT)
    total_a, held[PP], held[MM], held[Y1] = together(total_a, held[PP], held[MM], held[Y1])

    held[Y2] = send(held[PP], FROM_OTHER)
    keep, given = products(table_b, [held[n] for n in HELD_B], HELD_B, PAIRS_B, (NX, NX))
    own_b, right_b, left_b = near(keep, send(given, CORE_SWAP))
    own_b, right_b, left_b = together(own_b, right_b, left_b)

    total_b = own_b + send(right_b, FROM_LEFT) + send(left_b, FROM_RIGHT)
    total_b, held[Y2] = together(total_b, held[Y2])

    has_first = jnp.asarray(first)[aux, blk]
    done = jnp.where(has_first, total_a, total_b) + send(jnp.where(has_first, total_b, total_a), Y_SWAP)
    (part_c,) = products(table_c, [held[n] for n in HELD_C], HELD_C, PAIRS_C, (1,))
    part_c = one_far(one_core(part_c[0], target_c), target_c)
    done, part_c = together(done, part_c)
    part_c = one_near(part_c, target_c)
    done, part_c = together(done, part_c)

    top = send(done, final[0]) + send(part_c, final_c[0, 0]) + send(part_c, final_c[1, 0])
    bottom = send(done, final[1]) + send(part_c, final_c[0, 1]) + send(part_c, final_c[1, 1])
    return jnp.concatenate([top, bottom], 0)


def solution(mesh):
    placed = (P("aux", "blk", None),)
    return jax.shard_map(
        per_device, mesh=mesh, in_specs=placed, out_specs=P("blk", "aux"), check_vma=False
    )
```

```python
import collections
import functools
import random

import jax
import jax.numpy as jnp
import numpy as np
from jax import lax
from jax.experimental import pallas as pl
from jax.experimental.pallas import tpu as pltpu
from jax.sharding import PartitionSpec as P

ALL = ("aux", "blk")
NX, NZ, GROUPS = 4, 8, 16
VMEM_LIMIT = 16 * 2**20


def device(y_lo, x, core, blk):
    return ((y_lo * NX + x % NX) * 2 + core) * GROUPS + blk


def block(h, z):
    return h % 2 * NZ + z % NZ


def every(move):
    return [
        (device(*move(y_lo, x, core, h, z)), device(y_lo, x, core, block(h, z)))
        for y_lo in range(2)
        for x in range(NX)
        for core in range(2)
        for h in range(2)
        for z in range(NZ)
    ]


def send(value, pairs):
    return lax.ppermute(value, ALL, pairs)


O, PZ, MZ, Y0 = (0, 0), (0, 1), (0, -1), (1, 0)
PP, MM, Y1, Y2 = (0, 2), (0, -2), (1, 1), (1, 2)
HELD_A = (O, PZ, MZ, Y0)
HELD_B = (O, MZ, PP, MM, Y1)
HELD_C = (MM, Y2)


def units_of(pairs, h, z):
    found = []
    for at, (first, second, halves) in enumerate(pairs):
        i, j = block(h + first[0], z + first[1]), block(h + second[0], z + second[1])
        for half in halves(h, z):
            core = half if halves is both else int(first == second)
            found.append(((at, int(i > j), core), min(i, j), max(i, j), half))
    return found


def both(h, z):
    return (0, 1)


def by_h(h, z):
    return (h,)


def by_z(h, z):
    return (0,) if 2 <= z < 6 else (1,)


def upper(h, z):
    return (0,)


def lower(h, z):
    return (1,)


PAIRS_A = ((O, PZ, both), (MZ, PZ, both), (O, Y0, by_h), (MZ, Y0, both), (O, O, upper))
PAIRS_B = ((MZ, PP, both), (MM, PP, by_z), (MZ, Y1, both), (MM, Y1, both), (O, O, lower))
PAIRS_C = ((MM, Y2, by_h),)


def steps(a, b, n):
    ahead, back = (b - a) % n, (a - b) % n
    share = 0.5 if ahead == back else 1.0
    found = []
    if ahead and ahead <= back:
        found += [((a + i) % n, 1, share) for i in range(ahead)]
    if ahead and back <= ahead:
        found += [((a - i) % n, -1, share) for i in range(back)]
    return found


@functools.cache
def route(source, target):
    found = []
    for weight, order in ((0.05, (0, 1, 2)), (1.0, (2, 1, 0))):
        at = list(source)
        for axis in order:
            for place, way, share in steps(at[axis], target[axis], (NX, 4, NZ)[axis]):
                link = at[:axis] + [place] + at[axis + 1 :]
                found.append(((weight, axis, way, *link), share))
            at[axis] = target[axis]
    return found


def links(own, place, y, unit):
    h, z = own // NZ, own % NZ
    _, row, col, _ = unit
    return route((place // 2, 2 * h + y, z), (col // 2 % NX, row // NZ * 2 + col // NZ, row % NZ))


def by_core(units):
    cores = [[index for index, unit in enumerate(units) if unit[0][2] == core] for core in (0, 1)]
    return [cores[place % 2][place // 2] for place in range(8)]


@functools.cache
def spread(trials=40000):
    draw = random.Random(0)
    where = [(own // NZ, own % NZ) for own in range(GROUPS)]
    units = [[units_of(pairs, h, z) for pairs in (PAIRS_A, PAIRS_B)] for h, z in where]
    at = [[by_core(batch) for batch in both_batches] for both_batches in units]
    planes = [[h] * 8 for h, _ in where]
    load = collections.Counter()

    def on(own, batch, place, index, y):
        return links(own, place, 1 - y if batch else y, units[own][batch][index])

    for own, (h, z) in enumerate(where):
        for batch in (0, 1):
            for place in range(8):
                for link, share in on(own, batch, place, at[own][batch][place], planes[own][place]):
                    load[link] += share
        for unit in units_of(PAIRS_C, h, z):
            for y in (0, 1):
                for link, share in links(own, unit[2] % 8, y, unit):
                    load[link] += share
    for _ in range(trials):
        own, batch, u, v = draw.randrange(GROUPS), draw.randrange(2), draw.randrange(8), draw.randrange(8)
        if (u - v) % 2:
            continue
        now, plane = at[own], planes[own]
        change = collections.Counter()
        if u == v:
            for one in (0, 1):
                for sign, y in ((-1, plane[u]), (1, 1 - plane[u])):
                    for link, share in on(own, one, u, now[one][u], y):
                        change[link] += sign * share
        else:
            i, j = now[batch][u], now[batch][v]
            for sign, place, index in ((-1, u, i), (-1, v, j), (1, u, j), (1, v, i)):
                for link, share in on(own, batch, place, index, plane[place]):
                    change[link] += sign * share
        if sum(link[0] * ((load[link] + d) ** 4 - load[link] ** 4) for link, d in change.items()) <= 0:
            for link, d in change.items():
                load[link] += d
            if u == v:
                plane[u] = 1 - plane[u]
            else:
                now[batch][u], now[batch][v] = j, i
    return units, at, planes


@functools.cache
def plan():
    tables = np.zeros((2, 16, GROUPS, 5, 4), np.int32)
    table_c = np.zeros((GROUPS, 4), np.int32)
    target_c = {}
    final = {half: [] for half in (0, 1)}
    final_c = {(y, half): [] for y in (0, 1) for half in (0, 1)}
    first = np.zeros((16, GROUPS), np.bool_)
    units, at, planes = spread()
    for h in range(2):
        for z in range(NZ):
            own = block(h, z)
            for place in range(8):
                x, core = place // 2, place % 2
                for batch in range(2):
                    (pair, swap, _), row, col, half = units[own][batch][at[own][batch][place]]
                    y = 1 - planes[own][place] if batch else planes[own][place]
                    final[half].append((device(y, x, core, own), col * GROUPS + row))
                    first[(y * NX + x) * 2 + core, own] = not batch
                    for aux in range(16):
                        entry, offset = tables[batch, aux, own, pair], (x - aux // 2) % NX
                        kept = aux % 2 == core
                        entry[0] = swap
                        if (PAIRS_A, PAIRS_B)[batch][pair][2] is both:
                            entry[1 if kept else 2] = offset
                            entry[3] = aux % 2
                        else:
                            entry[1:] = offset, kept, half
            (((_, swap, _), row, col, half),) = units_of(PAIRS_C, h, z)
            table_c[own] = swap, 0, 1, half
            target_c[own] = (1 - h, col // 2 % NX, col % 2)
            for y in (0, 1):
                final_c[y, half].append((device(y, *target_c[own][1:], own), col * GROUPS + row))
    return tables.reshape(2, 16 * GROUPS, 20), table_c, target_c, first, final, final_c


def dot_t(a, b):
    return lax.dot_general(a, b, (((1,), (1,)), ((), ())), preferred_element_type=jnp.float32)


def half_product(rows, cols, half):
    at = pl.ds(pl.multiple_of(half * 256, 256), 256)
    total = dot_t(rows[0, at, :], cols[0])
    for k in range(1, rows.shape[0]):
        total += dot_t(rows[k, at, :], cols[k])
    return total


def units_kernel(pairs, index_pairs, spare, table, *refs):
    held, outs = refs[: len(refs) - spare], refs[len(refs) - spare :]
    for at, ((first, second), (_, _, halves)) in enumerate(zip(index_pairs, pairs)):
        swap, one, two, half = (table[4 * at + i] for i in range(4))
        for turned in range(1 if first == second else 2):
            rows, cols = (held[second], held[first]) if turned else (held[first], held[second])
            if halves is both:

                @pl.when(swap == turned)
                def _():
                    outs[1][two] = half_product(rows, cols, 1 - half)
                    outs[0][one] = half_product(rows, cols, half)

            else:
                for mine in range(2 - len(outs), 2):

                    @pl.when((swap == turned) & (two == mine))
                    def _():
                        outs[1 - mine][one] = half_product(rows, cols, half)


def products(table, held, names, pairs, counts):
    index_pairs = tuple((names.index(a), names.index(b)) for a, b, _ in pairs)
    return pl.pallas_call(
        functools.partial(units_kernel, pairs, index_pairs, len(counts)),
        out_shape=[pltpu.VMEM((count, 256, 512), jnp.float32) for count in counts],
        in_specs=[pl.BlockSpec(memory_space=pltpu.SMEM)]
        + [pl.BlockSpec(memory_space=pltpu.VMEM)] * len(held),
        out_specs=[pl.BlockSpec(memory_space=pltpu.VMEM)] * len(counts),
        compiler_params=pltpu.CompilerParams(vmem_limit_bytes=VMEM_LIMIT),
    )(table, *held)


def toward(targets, source, only):
    return [
        (device(*source(y, x, c, step), b), device(*only(y, x, c, step), b))
        for b, (y, x, c) in targets.items()
        for step in range(8)
    ]


def copy_kernel(source, out):
    out[...] = source[...]


def placed(value):
    return pl.pallas_call(
        copy_kernel,
        out_shape=pltpu.VMEM(value.shape, value.dtype),
        in_specs=[pl.BlockSpec(memory_space=pltpu.VMEM)],
        out_specs=pl.BlockSpec(memory_space=pltpu.VMEM),
        compiler_params=pltpu.CompilerParams(vmem_limit_bytes=VMEM_LIMIT),
    )(value)


def one_core(value, targets):
    def at(core_of):
        return lambda y, x, c, step: (step // NX, x + step % NX, core_of(c))

    return value + send(value, toward(targets, at(lambda c: 1 - c), at(lambda c: c)))


def along(targets, offset_from, offset_to):
    def at(offset):
        return lambda y, x, c, step: (step % 2, x + offset, c)

    return sorted(set(toward(targets, at(offset_from), at(offset_to))))


def one_x(value, targets):
    parts = [send(value, along(targets, offset, 0)) for offset in (2, 1, 3)]
    return value + parts[0] + (parts[1] + parts[2])


Y_SWAP = every(lambda y, x, c, h, z: (1 - y, x, c, block(h, z)))
CORE_SWAP = every(lambda y, x, c, h, z: (y, x, 1 - c, block(h, z)))
FROM_LEFT = every(lambda y, x, c, h, z: (y, x - 1, c, block(h, z)))
FROM_RIGHT = every(lambda y, x, c, h, z: (y, x + 1, c, block(h, z)))
FROM_UP = every(lambda y, x, c, h, z: (y, x, c, block(h, z + 1)))
FROM_DOWN = every(lambda y, x, c, h, z: (y, x, c, block(h, z - 1)))
FROM_OTHER = every(lambda y, x, c, h, z: (y, x, c, block(h + 1, z)))


def near(keep, got):
    middle = keep.shape[1] // 2
    far_top = send(keep[2, :middle] + got[2, :middle], FROM_LEFT)
    far_bottom = send(keep[2, middle:] + got[2, middle:], FROM_RIGHT)
    right = keep[1] + got[1]
    right = jnp.concatenate([right[:middle] + far_top, right[middle:]], 0)
    left = keep[3] + got[3]
    left = jnp.concatenate([left[:middle], left[middle:] + far_bottom], 0)
    return keep[0] + got[0], right, left


def together(*values):
    return lax.optimization_barrier(values)


def per_device(half_b):
    local, codes_c, target_c, first, final, final_c = plan()
    aux, blk = lax.axis_index("aux"), lax.axis_index("blk")
    place = aux * GROUPS + blk
    table_a, table_b = jnp.asarray(local[0])[place], jnp.asarray(local[1])[place]
    table_c = jnp.asarray(codes_c)[blk]

    held = {O: placed(half_b)}
    held[PZ] = send(half_b, FROM_UP)
    held[MZ] = send(half_b, FROM_DOWN)
    held[Y0] = send(half_b, FROM_OTHER)
    held[O], held[PZ], held[MZ], held[Y0] = together(held[O], held[PZ], held[MZ], held[Y0])

    held[PP] = send(held[PZ], FROM_UP)
    held[MM] = send(held[MZ], FROM_DOWN)
    held[Y1] = send(held[PZ], FROM_OTHER)
    keep, given = products(table_a, [held[n] for n in HELD_A], HELD_A, PAIRS_A, (NX, NX))
    own_a, right_a, left_a = near(keep, send(given, CORE_SWAP))
    total_a = own_a + send(right_a, FROM_LEFT) + send(left_a, FROM_RIGHT)
    total_a, held[PP], held[MM], held[Y1] = together(total_a, held[PP], held[MM], held[Y1])

    held[Y2] = send(held[PP], FROM_OTHER)
    keep, given = products(table_b, [held[n] for n in HELD_B], HELD_B, PAIRS_B, (NX, NX))
    own_b, right_b, left_b = near(keep, send(given, CORE_SWAP))
    own_b, right_b, left_b = together(own_b, right_b, left_b)

    total_b = own_b + send(right_b, FROM_LEFT) + send(left_b, FROM_RIGHT)
    total_b, held[Y2] = together(total_b, held[Y2])

    has_first = jnp.asarray(first)[aux, blk]
    done = jnp.where(has_first, total_a, total_b) + send(jnp.where(has_first, total_b, total_a), Y_SWAP)
    (part_c,) = products(table_c, [held[n] for n in HELD_C], HELD_C, PAIRS_C, (1,))
    part_c = one_x(one_core(part_c[0], target_c), target_c)
    done, part_c = together(done, part_c)

    top = send(done, final[0]) + send(part_c, final_c[0, 0]) + send(part_c, final_c[1, 0])
    bottom = send(done, final[1]) + send(part_c, final_c[0, 1]) + send(part_c, final_c[1, 1])
    return jnp.concatenate([top, bottom], 0)


def solution(mesh):
    placed = (P("aux", "blk", None),)
    return jax.shard_map(
        per_device, mesh=mesh, in_specs=placed, out_specs=P("blk", "aux"), check_vma=False
    )
```

```python
import collections
import functools
import random

import jax
import jax.numpy as jnp
import numpy as np
from jax import lax
from jax.experimental import pallas as pl
from jax.experimental.pallas import tpu as pltpu
from jax.sharding import PartitionSpec as P

ALL = ("aux", "blk")
NX, NZ, GROUPS = 4, 8, 16
VMEM_LIMIT = 16 * 2**20


def device(y_lo, x, core, blk):
    return ((y_lo * NX + x % NX) * 2 + core) * GROUPS + blk


def block(h, z):
    return h % 2 * NZ + z % NZ


def every(move):
    return [
        (device(*move(y_lo, x, core, h, z)), device(y_lo, x, core, block(h, z)))
        for y_lo in range(2)
        for x in range(NX)
        for core in range(2)
        for h in range(2)
        for z in range(NZ)
    ]


def send(value, pairs):
    return lax.ppermute(value, ALL, pairs)


O, PZ, MZ, Y0 = (0, 0), (0, 1), (0, -1), (1, 0)
PP, MM, Y1, Y2 = (0, 2), (0, -2), (1, 1), (1, 2)
HELD_A = (O, PZ, MZ, Y0)
HELD_B = (O, MZ, PP, MM, Y1)
HELD_C = (MM, Y2)


def units_of(pairs, h, z):
    found = []
    for at, (first, second, halves) in enumerate(pairs):
        i, j = block(h + first[0], z + first[1]), block(h + second[0], z + second[1])
        for half in halves(h, z):
            core = half if halves is both else int(first == second)
            found.append(((at, int(i > j), core), min(i, j), max(i, j), half))
    return found


def both(h, z):
    return (0, 1)


def by_h(h, z):
    return (h,)


def by_z(h, z):
    return (0,) if 2 <= z < 6 else (1,)


def upper(h, z):
    return (0,)


def lower(h, z):
    return (1,)


PAIRS_A = ((O, PZ, both), (MZ, PZ, both), (O, Y0, by_h), (MZ, Y0, both), (O, O, upper))
PAIRS_B = ((MZ, PP, both), (MM, PP, by_z), (MZ, Y1, both), (MM, Y1, both), (O, O, lower))
PAIRS_C = ((MM, Y2, by_h),)


def steps(a, b, n):
    ahead, back = (b - a) % n, (a - b) % n
    share = 0.5 if ahead == back else 1.0
    found = []
    if ahead and ahead <= back:
        found += [((a + i) % n, 1, share) for i in range(ahead)]
    if ahead and back <= ahead:
        found += [((a - i) % n, -1, share) for i in range(back)]
    return found


@functools.cache
def route(source, target):
    found = []
    for weight, order in ((1.0, (2, 0, 1)), (0.01, (2, 1, 0))):
        at = list(source)
        for axis in order:
            for place, way, share in steps(at[axis], target[axis], (NX, 4, NZ)[axis]):
                link = at[:axis] + [place] + at[axis + 1 :]
                found.append(((weight, axis, way, *link), share))
            at[axis] = target[axis]
    return found


def links(own, place, y, unit):
    h, z = own // NZ, own % NZ
    _, row, col, _ = unit
    return route((place // 2, 2 * h + y, z), (col // 2 % NX, row // NZ * 2 + col // NZ, row % NZ))


def by_core(units):
    cores = [[index for index, unit in enumerate(units) if unit[0][2] == core] for core in (0, 1)]
    return [cores[place % 2][place // 2] for place in range(8)]


@functools.cache
def spread(trials=120000):
    draw = random.Random(0)
    where = [(own // NZ, own % NZ) for own in range(GROUPS)]
    units = [[units_of(pairs, h, z) for pairs in (PAIRS_A, PAIRS_B)] for h, z in where]
    at = [[by_core(batch) for batch in both_batches] for both_batches in units]
    planes = [[h] * 8 for h, _ in where]
    load = collections.Counter()

    def on(own, batch, place, index, y):
        return links(own, place, 1 - y if batch else y, units[own][batch][index])

    for own, (h, z) in enumerate(where):
        for batch in (0, 1):
            for place in range(8):
                for link, share in on(own, batch, place, at[own][batch][place], planes[own][place]):
                    load[link] += share
        for unit in units_of(PAIRS_C, h, z):
            for y in (0, 1):
                for link, share in links(own, unit[2] % 8, y, unit):
                    load[link] += share
    for _ in range(trials):
        own, batch, u, v = draw.randrange(GROUPS), draw.randrange(2), draw.randrange(8), draw.randrange(8)
        if (u - v) % 2:
            continue
        now, plane = at[own], planes[own]
        change = collections.Counter()
        if u == v:
            for one in (0, 1):
                for sign, y in ((-1, plane[u]), (1, 1 - plane[u])):
                    for link, share in on(own, one, u, now[one][u], y):
                        change[link] += sign * share
        else:
            i, j = now[batch][u], now[batch][v]
            for sign, place, index in ((-1, u, i), (-1, v, j), (1, u, j), (1, v, i)):
                for link, share in on(own, batch, place, index, plane[place]):
                    change[link] += sign * share
        if sum(link[0] * ((load[link] + d) ** 6 - load[link] ** 6) for link, d in change.items()) <= 0:
            for link, d in change.items():
                load[link] += d
            if u == v:
                plane[u] = 1 - plane[u]
            else:
                now[batch][u], now[batch][v] = j, i
    return units, at, planes


@functools.cache
def plan():
    tables = np.zeros((2, 16, GROUPS, 5, 4), np.int32)
    table_c = np.zeros((GROUPS, 4), np.int32)
    target_c = {}
    final = {half: [] for half in (0, 1)}
    final_c = {(y, half): [] for y in (0, 1) for half in (0, 1)}
    first = np.zeros((16, GROUPS), np.bool_)
    units, at, planes = spread()
    for h in range(2):
        for z in range(NZ):
            own = block(h, z)
            for place in range(8):
                x, core = place // 2, place % 2
                for batch in range(2):
                    (pair, swap, _), row, col, half = units[own][batch][at[own][batch][place]]
                    y = 1 - planes[own][place] if batch else planes[own][place]
                    final[half].append((device(y, x, core, own), col * GROUPS + row))
                    first[(y * NX + x) * 2 + core, own] = not batch
                    for aux in range(16):
                        entry, offset = tables[batch, aux, own, pair], (x - aux // 2) % NX
                        kept = aux % 2 == core
                        entry[0] = swap
                        if (PAIRS_A, PAIRS_B)[batch][pair][2] is both:
                            entry[1 if kept else 2] = offset
                            entry[3] = aux % 2
                        else:
                            entry[1:] = offset, kept, half
            (((_, swap, _), row, col, half),) = units_of(PAIRS_C, h, z)
            table_c[own] = swap, 0, 1, half
            target_c[own] = (1 - h, col // 2 % NX, col % 2)
            for y in (0, 1):
                final_c[y, half].append((device(y, *target_c[own][1:], own), col * GROUPS + row))
    return tables.reshape(2, 16 * GROUPS, 20), table_c, target_c, first, final, final_c


def dot_t(a, b):
    return lax.dot_general(a, b, (((1,), (1,)), ((), ())), preferred_element_type=jnp.float32)


def half_product(rows, cols, half):
    at = pl.ds(pl.multiple_of(half * 256, 256), 256)
    total = dot_t(rows[0, at, :], cols[0])
    for k in range(1, rows.shape[0]):
        total += dot_t(rows[k, at, :], cols[k])
    return total


def units_kernel(pairs, index_pairs, spare, table, *refs):
    held, outs = refs[: len(refs) - spare], refs[len(refs) - spare :]
    for at, ((first, second), (_, _, halves)) in enumerate(zip(index_pairs, pairs)):
        swap, one, two, half = (table[4 * at + i] for i in range(4))
        for turned in range(1 if first == second else 2):
            rows, cols = (held[second], held[first]) if turned else (held[first], held[second])
            if halves is both:

                @pl.when(swap == turned)
                def _():
                    outs[1][two] = half_product(rows, cols, 1 - half)
                    outs[0][one] = half_product(rows, cols, half)

            else:
                for mine in range(2 - len(outs), 2):

                    @pl.when((swap == turned) & (two == mine))
                    def _():
                        outs[1 - mine][one] = half_product(rows, cols, half)


def products(table, held, names, pairs, counts):
    index_pairs = tuple((names.index(a), names.index(b)) for a, b, _ in pairs)
    return pl.pallas_call(
        functools.partial(units_kernel, pairs, index_pairs, len(counts)),
        out_shape=[pltpu.VMEM((count, 256, 512), jnp.float32) for count in counts],
        in_specs=[pl.BlockSpec(memory_space=pltpu.SMEM)]
        + [pl.BlockSpec(memory_space=pltpu.VMEM)] * len(held),
        out_specs=[pl.BlockSpec(memory_space=pltpu.VMEM)] * len(counts),
        compiler_params=pltpu.CompilerParams(vmem_limit_bytes=VMEM_LIMIT),
    )(table, *held)


def toward(targets, source, only):
    return [
        (device(*source(y, x, c, step), b), device(*only(y, x, c, step), b))
        for b, (y, x, c) in targets.items()
        for step in range(8)
    ]


def copy_kernel(source, out):
    out[...] = source[...]


def placed(value):
    return pl.pallas_call(
        copy_kernel,
        out_shape=pltpu.VMEM(value.shape, value.dtype),
        in_specs=[pl.BlockSpec(memory_space=pltpu.VMEM)],
        out_specs=pl.BlockSpec(memory_space=pltpu.VMEM),
        compiler_params=pltpu.CompilerParams(vmem_limit_bytes=VMEM_LIMIT),
    )(value)


def one_core(value, targets):
    def at(core_of):
        return lambda y, x, c, step: (step // NX, x + step % NX, core_of(c))

    return value + send(value, toward(targets, at(lambda c: 1 - c), at(lambda c: c)))


def along(targets, offset_from, offset_to):
    def at(offset):
        return lambda y, x, c, step: (step % 2, x + offset, c)

    return sorted(set(toward(targets, at(offset_from), at(offset_to))))


def one_x(value, targets):
    parts = [send(value, along(targets, offset, 0)) for offset in (2, 1, 3)]
    return value + parts[0] + (parts[1] + parts[2])


Y_SWAP = every(lambda y, x, c, h, z: (1 - y, x, c, block(h, z)))
CORE_SWAP = every(lambda y, x, c, h, z: (y, x, 1 - c, block(h, z)))
FROM_LEFT = every(lambda y, x, c, h, z: (y, x - 1, c, block(h, z)))
FROM_RIGHT = every(lambda y, x, c, h, z: (y, x + 1, c, block(h, z)))
FROM_UP = every(lambda y, x, c, h, z: (y, x, c, block(h, z + 1)))
FROM_DOWN = every(lambda y, x, c, h, z: (y, x, c, block(h, z - 1)))
FROM_OTHER = every(lambda y, x, c, h, z: (y, x, c, block(h + 1, z)))


def near(keep, got):
    middle = keep.shape[1] // 2
    far_top = send(keep[2, :middle] + got[2, :middle], FROM_LEFT)
    far_bottom = send(keep[2, middle:] + got[2, middle:], FROM_RIGHT)
    right = keep[1] + got[1]
    right = jnp.concatenate([right[:middle] + far_top, right[middle:]], 0)
    left = keep[3] + got[3]
    left = jnp.concatenate([left[:middle], left[middle:] + far_bottom], 0)
    return keep[0] + got[0], right, left


def together(*values):
    return lax.optimization_barrier(values)


def per_device(half_b):
    local, codes_c, target_c, first, final, final_c = plan()
    aux, blk = lax.axis_index("aux"), lax.axis_index("blk")
    place = aux * GROUPS + blk
    table_a, table_b = jnp.asarray(local[0])[place], jnp.asarray(local[1])[place]
    table_c = jnp.asarray(codes_c)[blk]

    held = {O: placed(half_b)}
    held[PZ] = send(half_b, FROM_UP)
    held[MZ] = send(half_b, FROM_DOWN)
    held[Y0] = send(half_b, FROM_OTHER)
    held[O], held[PZ], held[MZ], held[Y0] = together(held[O], held[PZ], held[MZ], held[Y0])

    held[PP] = send(held[PZ], FROM_UP)
    held[MM] = send(held[MZ], FROM_DOWN)
    held[Y1] = send(held[PZ], FROM_OTHER)
    keep, given = products(table_a, [held[n] for n in HELD_A], HELD_A, PAIRS_A, (NX, NX))
    own_a, right_a, left_a = near(keep, send(given, CORE_SWAP))
    total_a = own_a + send(right_a, FROM_LEFT) + send(left_a, FROM_RIGHT)
    total_a, held[PP], held[MM], held[Y1] = together(total_a, held[PP], held[MM], held[Y1])

    held[Y2] = send(held[PP], FROM_OTHER)
    keep, given = products(table_b, [held[n] for n in HELD_B], HELD_B, PAIRS_B, (NX, NX))
    own_b, right_b, left_b = near(keep, send(given, CORE_SWAP))
    own_b, right_b, left_b = together(own_b, right_b, left_b)

    total_b = own_b + send(right_b, FROM_LEFT) + send(left_b, FROM_RIGHT)
    total_b, held[Y2] = together(total_b, held[Y2])

    has_first = jnp.asarray(first)[aux, blk]
    done = jnp.where(has_first, total_a, total_b) + send(jnp.where(has_first, total_b, total_a), Y_SWAP)
    (part_c,) = products(table_c, [held[n] for n in HELD_C], HELD_C, PAIRS_C, (1,))
    part_c = one_x(one_core(part_c[0], target_c), target_c)
    done, part_c = together(done, part_c)

    top = send(done, final[0]) + send(part_c, final_c[0, 0]) + send(part_c, final_c[1, 0])
    bottom = send(done, final[1]) + send(part_c, final_c[0, 1]) + send(part_c, final_c[1, 1])
    return jnp.concatenate([top, bottom], 0)


def solution(mesh):
    placed = (P("aux", "blk", None),)
    return jax.shard_map(
        per_device, mesh=mesh, in_specs=placed, out_specs=P("blk", "aux"), check_vma=False
    )
```

```python
import collections
import functools
import random

import jax
import jax.numpy as jnp
import numpy as np
from jax import lax
from jax.experimental import pallas as pl
from jax.experimental.pallas import tpu as pltpu
from jax.sharding import PartitionSpec as P

ALL = ("aux", "blk")
NX, NZ, GROUPS = 4, 8, 16
VMEM_LIMIT = 16 * 2**20


def device(y_lo, x, core, blk):
    return ((y_lo * NX + x % NX) * 2 + core) * GROUPS + blk


def block(h, z):
    return h % 2 * NZ + z % NZ


def every(move):
    return [
        (device(*move(y_lo, x, core, h, z)), device(y_lo, x, core, block(h, z)))
        for y_lo in range(2)
        for x in range(NX)
        for core in range(2)
        for h in range(2)
        for z in range(NZ)
    ]


def send(value, pairs):
    return lax.ppermute(value, ALL, pairs)


O, PZ, MZ, Y0 = (0, 0), (0, 1), (0, -1), (1, 0)
PP, MM, Y1, Y2 = (0, 2), (0, -2), (1, 1), (1, 2)
HELD_A = (O, PZ, MZ, Y0)
HELD_B = (O, MZ, PP, MM, Y1)
HELD_C = (MM, Y2)


def units_of(pairs, h, z):
    found = []
    for at, (first, second, halves) in enumerate(pairs):
        i, j = block(h + first[0], z + first[1]), block(h + second[0], z + second[1])
        for half in halves(h, z):
            core = half if halves is both else int(first == second)
            found.append(((at, int(i > j), core), min(i, j), max(i, j), half))
    return found


def both(h, z):
    return (0, 1)


def by_h(h, z):
    return (h,)


def by_z(h, z):
    return (0,) if 2 <= z < 6 else (1,)


def upper(h, z):
    return (0,)


def lower(h, z):
    return (1,)


PAIRS_A = ((O, PZ, both), (MZ, PZ, both), (O, Y0, by_h), (MZ, Y0, both), (O, O, upper))
PAIRS_B = ((MZ, PP, both), (MM, PP, by_z), (MZ, Y1, both), (MM, Y1, both), (O, O, lower))
PAIRS_C = ((MM, Y2, by_h),)


def steps(a, b, n):
    ahead, back = (b - a) % n, (a - b) % n
    share = 0.5 if ahead == back else 1.0
    found = []
    if ahead and ahead <= back:
        found += [((a + i) % n, 1, share) for i in range(ahead)]
    if ahead and back <= ahead:
        found += [((a - i) % n, -1, share) for i in range(back)]
    return found


@functools.cache
def route(source, target):
    found = []
    for weight, order in ((1.0, (2, 0, 1)), (0.01, (2, 1, 0))):
        at = list(source)
        for axis in order:
            for place, way, share in steps(at[axis], target[axis], (NX, 4, NZ)[axis]):
                link = at[:axis] + [place] + at[axis + 1 :]
                found.append(((weight, axis, way, *link), share))
            at[axis] = target[axis]
    return found


def links(own, place, y, unit):
    h, z = own // NZ, own % NZ
    _, row, col, _ = unit
    return route((place // 2, 2 * h + y, z), (col // 2 % NX, row // NZ * 2 + col // NZ, row % NZ))


def by_core(units):
    cores = [[index for index, unit in enumerate(units) if unit[0][2] == core] for core in (0, 1)]
    return [cores[place % 2][place // 2] for place in range(8)]


@functools.cache
def spread(trials=120000):
    draw = random.Random(0)
    where = [(own // NZ, own % NZ) for own in range(GROUPS)]
    units = [[units_of(pairs, h, z) for pairs in (PAIRS_A, PAIRS_B)] for h, z in where]
    at = [[by_core(batch) for batch in both_batches] for both_batches in units]
    planes = [[h] * 8 for h, _ in where]
    load = collections.Counter()

    def on(own, batch, place, index, y):
        return links(own, place, 1 - y if batch else y, units[own][batch][index])

    for own, (h, z) in enumerate(where):
        for batch in (0, 1):
            for place in range(8):
                for link, share in on(own, batch, place, at[own][batch][place], planes[own][place]):
                    load[link] += share
        for unit in units_of(PAIRS_C, h, z):
            for y in (0, 1):
                for link, share in links(own, unit[2] % 8, y, unit):
                    load[link] += share
    for _ in range(trials):
        own, batch, u, v = draw.randrange(GROUPS), draw.randrange(2), draw.randrange(8), draw.randrange(8)
        if (u - v) % 2:
            continue
        now, plane = at[own], planes[own]
        change = collections.Counter()
        if u == v:
            for one in (0, 1):
                for sign, y in ((-1, plane[u]), (1, 1 - plane[u])):
                    for link, share in on(own, one, u, now[one][u], y):
                        change[link] += sign * share
        else:
            i, j = now[batch][u], now[batch][v]
            for sign, place, index in ((-1, u, i), (-1, v, j), (1, u, j), (1, v, i)):
                for link, share in on(own, batch, place, index, plane[place]):
                    change[link] += sign * share
        if sum(link[0] * ((load[link] + d) ** 6 - load[link] ** 6) for link, d in change.items()) <= 0:
            for link, d in change.items():
                load[link] += d
            if u == v:
                plane[u] = 1 - plane[u]
            else:
                now[batch][u], now[batch][v] = j, i
    return units, at, planes


@functools.cache
def plan():
    tables = np.zeros((2, 16, GROUPS, 5, 4), np.int32)
    table_c = np.zeros((GROUPS, 4), np.int32)
    target_c = {}
    final = {half: [] for half in (0, 1)}
    final_c = {half: [] for half in (0, 1)}
    halves = np.zeros((16, GROUPS), np.int32)
    first = np.zeros((16, GROUPS), np.bool_)
    units, at, planes = spread()
    for h in range(2):
        for z in range(NZ):
            own = block(h, z)
            for place in range(8):
                x, core = place // 2, place % 2
                for batch in range(2):
                    (pair, swap, _), row, col, half = units[own][batch][at[own][batch][place]]
                    y = 1 - planes[own][place] if batch else planes[own][place]
                    final[half].append((device(y, x, core, own), col * GROUPS + row))
                    first[(y * NX + x) * 2 + core, own] = not batch
                    halves[(y * NX + x) * 2 + core, own] = half
                    for aux in range(16):
                        entry, offset = tables[batch, aux, own, pair], (x - aux // 2) % NX
                        kept = aux % 2 == core
                        entry[0] = swap
                        if (PAIRS_A, PAIRS_B)[batch][pair][2] is both:
                            entry[1 if kept else 2] = offset
                            entry[3] = aux % 2
                        else:
                            entry[1:] = offset, kept, half
            (((_, swap, _), row, col, half),) = units_of(PAIRS_C, h, z)
            table_c[own] = swap, 0, 1, half
            y, x, core = min(
                ((y, x, core) for y in (0, 1) for x in range(NX) for core in (0, 1)
                 if halves[(y * NX + x) * 2 + core, own] != half),
                key=lambda place: (min((place[1] - col // 2) % NX, (col // 2 - place[1]) % NX), place),
            )
            target_c[own] = (y, x, core)
            final[half].append((device(y, x, core, own), col * GROUPS + row))
            final_c[half].append((device(1 - y, x, core, own), col * GROUPS + row))
    return tables.reshape(2, 16 * GROUPS, 20), table_c, target_c, first, halves, final, final_c


def dot_t(a, b):
    return lax.dot_general(a, b, (((1,), (1,)), ((), ())), preferred_element_type=jnp.float32)


def half_product(rows, cols, half):
    at = pl.ds(pl.multiple_of(half * 256, 256), 256)
    total = dot_t(rows[0, at, :], cols[0])
    for k in range(1, rows.shape[0]):
        total += dot_t(rows[k, at, :], cols[k])
    return total


def units_kernel(pairs, index_pairs, spare, table, *refs):
    held, outs = refs[: len(refs) - spare], refs[len(refs) - spare :]
    for at, ((first, second), (_, _, halves)) in enumerate(zip(index_pairs, pairs)):
        swap, one, two, half = (table[4 * at + i] for i in range(4))
        for turned in range(1 if first == second else 2):
            rows, cols = (held[second], held[first]) if turned else (held[first], held[second])
            if halves is both:

                @pl.when(swap == turned)
                def _():
                    outs[1][two] = half_product(rows, cols, 1 - half)
                    outs[0][one] = half_product(rows, cols, half)

            else:
                for mine in range(2 - len(outs), 2):

                    @pl.when((swap == turned) & (two == mine))
                    def _():
                        outs[1 - mine][one] = half_product(rows, cols, half)


def products(table, held, names, pairs, counts):
    index_pairs = tuple((names.index(a), names.index(b)) for a, b, _ in pairs)
    return pl.pallas_call(
        functools.partial(units_kernel, pairs, index_pairs, len(counts)),
        out_shape=[pltpu.VMEM((count, 256, 512), jnp.float32) for count in counts],
        in_specs=[pl.BlockSpec(memory_space=pltpu.SMEM)]
        + [pl.BlockSpec(memory_space=pltpu.VMEM)] * len(held),
        out_specs=[pl.BlockSpec(memory_space=pltpu.VMEM)] * len(counts),
        compiler_params=pltpu.CompilerParams(vmem_limit_bytes=VMEM_LIMIT),
    )(table, *held)


def toward(targets, source, only):
    return [
        (device(*source(y, x, c, step), b), device(*only(y, x, c, step), b))
        for b, (y, x, c) in targets.items()
        for step in range(8)
    ]


def copy_kernel(source, out):
    out[...] = source[...]


def placed(value):
    return pl.pallas_call(
        copy_kernel,
        out_shape=pltpu.VMEM(value.shape, value.dtype),
        in_specs=[pl.BlockSpec(memory_space=pltpu.VMEM)],
        out_specs=pl.BlockSpec(memory_space=pltpu.VMEM),
        compiler_params=pltpu.CompilerParams(vmem_limit_bytes=VMEM_LIMIT),
    )(value)


def one_core(value, targets):
    def at(core_of):
        return lambda y, x, c, step: (step // NX, x + step % NX, core_of(c))

    return value + send(value, toward(targets, at(lambda c: 1 - c), at(lambda c: c)))


def along(targets, offset_from, offset_to):
    def at(offset):
        return lambda y, x, c, step: (step % 2, x + offset, c)

    return sorted(set(toward(targets, at(offset_from), at(offset_to))))


def one_x(value, targets):
    parts = [send(value, along(targets, offset, 0)) for offset in (2, 1, 3)]
    return value + parts[0] + (parts[1] + parts[2])


Y_SWAP = every(lambda y, x, c, h, z: (1 - y, x, c, block(h, z)))
CORE_SWAP = every(lambda y, x, c, h, z: (y, x, 1 - c, block(h, z)))
FROM_LEFT = every(lambda y, x, c, h, z: (y, x - 1, c, block(h, z)))
FROM_RIGHT = every(lambda y, x, c, h, z: (y, x + 1, c, block(h, z)))
FROM_UP = every(lambda y, x, c, h, z: (y, x, c, block(h, z + 1)))
FROM_DOWN = every(lambda y, x, c, h, z: (y, x, c, block(h, z - 1)))
FROM_OTHER = every(lambda y, x, c, h, z: (y, x, c, block(h + 1, z)))


def near(keep, got):
    middle = keep.shape[1] // 2
    far_top = send(keep[2, :middle] + got[2, :middle], FROM_LEFT)
    far_bottom = send(keep[2, middle:] + got[2, middle:], FROM_RIGHT)
    right = keep[1] + got[1]
    right = jnp.concatenate([right[:middle] + far_top, right[middle:]], 0)
    left = keep[3] + got[3]
    left = jnp.concatenate([left[:middle], left[middle:] + far_bottom], 0)
    return keep[0] + got[0], right, left


def together(*values):
    return lax.optimization_barrier(values)


def per_device(half_b):
    local, codes_c, target_c, first, halves, final, final_c = plan()
    aux, blk = lax.axis_index("aux"), lax.axis_index("blk")
    place = aux * GROUPS + blk
    table_a, table_b = jnp.asarray(local[0])[place], jnp.asarray(local[1])[place]
    table_c = jnp.asarray(codes_c)[blk]

    held = {O: placed(half_b)}
    held[PZ] = send(half_b, FROM_UP)
    held[MZ] = send(half_b, FROM_DOWN)
    held[Y0] = send(half_b, FROM_OTHER)
    held[O], held[PZ], held[MZ], held[Y0] = together(held[O], held[PZ], held[MZ], held[Y0])

    held[PP] = send(held[PZ], FROM_UP)
    held[MM] = send(held[MZ], FROM_DOWN)
    held[Y1] = send(held[PZ], FROM_OTHER)
    keep, given = products(table_a, [held[n] for n in HELD_A], HELD_A, PAIRS_A, (NX, NX))
    own_a, right_a, left_a = near(keep, send(given, CORE_SWAP))
    total_a = own_a + send(right_a, FROM_LEFT) + send(left_a, FROM_RIGHT)
    total_a, held[PP], held[MM], held[Y1] = together(total_a, held[PP], held[MM], held[Y1])

    held[Y2] = send(held[PP], FROM_OTHER)
    keep, given = products(table_b, [held[n] for n in HELD_B], HELD_B, PAIRS_B, (NX, NX))
    own_b, right_b, left_b = near(keep, send(given, CORE_SWAP))
    own_b, right_b, left_b = together(own_b, right_b, left_b)

    total_b = own_b + send(right_b, FROM_LEFT) + send(left_b, FROM_RIGHT)
    total_b, held[Y2] = together(total_b, held[Y2])

    has_first = jnp.asarray(first)[aux, blk]
    done = jnp.where(has_first, total_a, total_b) + send(jnp.where(has_first, total_b, total_a), Y_SWAP)
    (part_c,) = products(table_c, [held[n] for n in HELD_C], HELD_C, PAIRS_C, (1,))
    part_c = one_x(one_core(part_c[0], target_c), target_c)
    done, part_c = together(done, part_c)

    own_half = jnp.asarray(halves)[aux, blk]
    top = send(jnp.where(own_half == 0, done, part_c), final[0]) + send(part_c, final_c[0])
    bottom = send(jnp.where(own_half == 1, done, part_c), final[1]) + send(part_c, final_c[1])
    return jnp.concatenate([top, bottom], 0)


def solution(mesh):
    placed = (P("aux", "blk", None),)
    return jax.shard_map(
        per_device, mesh=mesh, in_specs=placed, out_specs=P("blk", "aux"), check_vma=False
    )
```

```python
import collections
import functools
import random

import jax
import jax.numpy as jnp
import numpy as np
from jax import lax
from jax.experimental import pallas as pl
from jax.experimental.pallas import tpu as pltpu
from jax.sharding import PartitionSpec as P

ALL = ("aux", "blk")
NX, NZ, GROUPS = 4, 8, 16
VMEM_LIMIT = 16 * 2**20


def device(y_lo, x, core, blk):
    return ((y_lo * NX + x % NX) * 2 + core) * GROUPS + blk


def block(h, z):
    return h % 2 * NZ + z % NZ


def every(move):
    return [
        (device(*move(y_lo, x, core, h, z)), device(y_lo, x, core, block(h, z)))
        for y_lo in range(2)
        for x in range(NX)
        for core in range(2)
        for h in range(2)
        for z in range(NZ)
    ]


def send(value, pairs):
    return lax.ppermute(value, ALL, pairs)


O, PZ, MZ, Y0 = (0, 0), (0, 1), (0, -1), (1, 0)
PP, MM, Y1, Y2 = (0, 2), (0, -2), (1, 1), (1, 2)
HELD_A = (O, PZ, MZ, Y0)
HELD_B = (O, MZ, PP, MM, Y1)
HELD_C = (MM, Y2)


def units_of(pairs, h, z):
    found = []
    for at, (first, second, halves) in enumerate(pairs):
        i, j = block(h + first[0], z + first[1]), block(h + second[0], z + second[1])
        for half in halves(h, z):
            core = half if halves is both else int(first == second)
            found.append(((at, int(i > j), core), min(i, j), max(i, j), half))
    return found


def both(h, z):
    return (0, 1)


def by_h(h, z):
    return (h,)


def by_z(h, z):
    return (0,) if 2 <= z < 6 else (1,)


def upper(h, z):
    return (0,)


def lower(h, z):
    return (1,)


PAIRS_A = ((O, PZ, both), (MZ, PZ, both), (O, Y0, by_h), (MZ, Y0, both), (O, O, upper))
PAIRS_B = ((MZ, PP, both), (MM, PP, by_z), (MZ, Y1, both), (MM, Y1, both), (O, O, lower))
PAIRS_C = ((MM, Y2, by_h),)


def steps(a, b, n):
    ahead, back = (b - a) % n, (a - b) % n
    found = []
    if ahead and ahead <= back:
        found += [((a + i) % n, 1, 1.0) for i in range(ahead)]
    if ahead and back <= ahead:
        found += [((a - i) % n, -1, 1.0) for i in range(back)]
    return found


@functools.cache
def route(source, target):
    found = []
    for weight, order in ((1.0, (2, 0, 1)), (0.01, (2, 1, 0))):
        at = list(source)
        for axis in order:
            for place, way, share in steps(at[axis], target[axis], (NX, 4, NZ)[axis]):
                link = at[:axis] + [place] + at[axis + 1 :]
                found.append(((weight, axis, way, *link), share))
            at[axis] = target[axis]
    return found


def links(own, place, y, unit):
    h, z = own // NZ, own % NZ
    _, row, col, _ = unit
    return route((place // 2, 2 * h + y, z), (col // 2 % NX, row // NZ * 2 + col // NZ, row % NZ))


def by_core(units):
    cores = [[index for index, unit in enumerate(units) if unit[0][2] == core] for core in (0, 1)]
    return [cores[place % 2][place // 2] for place in range(8)]


@functools.cache
def spread(trials=120000):
    draw = random.Random(0)
    where = [(own // NZ, own % NZ) for own in range(GROUPS)]
    units = [[units_of(pairs, h, z) for pairs in (PAIRS_A, PAIRS_B)] for h, z in where]
    at = [[by_core(batch) for batch in both_batches] for both_batches in units]
    planes = [[h] * 8 for h, _ in where]
    load = collections.Counter()

    def on(own, batch, place, index, y):
        return links(own, place, 1 - y if batch else y, units[own][batch][index])

    for own, (h, z) in enumerate(where):
        for batch in (0, 1):
            for place in range(8):
                for link, share in on(own, batch, place, at[own][batch][place], planes[own][place]):
                    load[link] += share
        for unit in units_of(PAIRS_C, h, z):
            for y in (0, 1):
                for link, share in links(own, unit[2] % 8, y, unit):
                    load[link] += share
    for _ in range(trials):
        own, batch, u, v = draw.randrange(GROUPS), draw.randrange(2), draw.randrange(8), draw.randrange(8)
        if (u - v) % 2:
            continue
        now, plane = at[own], planes[own]
        change = collections.Counter()
        if u == v:
            for one in (0, 1):
                for sign, y in ((-1, plane[u]), (1, 1 - plane[u])):
                    for link, share in on(own, one, u, now[one][u], y):
                        change[link] += sign * share
        else:
            i, j = now[batch][u], now[batch][v]
            for sign, place, index in ((-1, u, i), (-1, v, j), (1, u, j), (1, v, i)):
                for link, share in on(own, batch, place, index, plane[place]):
                    change[link] += sign * share
        if sum(link[0] * ((load[link] + d) ** 6 - load[link] ** 6) for link, d in change.items()) <= 0:
            for link, d in change.items():
                load[link] += d
            if u == v:
                plane[u] = 1 - plane[u]
            else:
                now[batch][u], now[batch][v] = j, i
    return units, at, planes


@functools.cache
def plan():
    tables = np.zeros((2, 16, GROUPS, 5, 4), np.int32)
    table_c = np.zeros((GROUPS, 4), np.int32)
    target_c = {}
    final = {half: [] for half in (0, 1)}
    final_c = {half: [] for half in (0, 1)}
    halves = np.zeros((16, GROUPS), np.int32)
    first = np.zeros((16, GROUPS), np.bool_)
    units, at, planes = spread()
    for h in range(2):
        for z in range(NZ):
            own = block(h, z)
            for place in range(8):
                x, core = place // 2, place % 2
                for batch in range(2):
                    (pair, swap, _), row, col, half = units[own][batch][at[own][batch][place]]
                    y = 1 - planes[own][place] if batch else planes[own][place]
                    final[half].append((device(y, x, core, own), col * GROUPS + row))
                    first[(y * NX + x) * 2 + core, own] = not batch
                    halves[(y * NX + x) * 2 + core, own] = half
                    for aux in range(16):
                        entry, offset = tables[batch, aux, own, pair], (x - aux // 2) % NX
                        kept = aux % 2 == core
                        entry[0] = swap
                        if (PAIRS_A, PAIRS_B)[batch][pair][2] is both:
                            entry[1 if kept else 2] = offset
                            entry[3] = aux % 2
                        else:
                            entry[1:] = offset, kept, half
            (((_, swap, _), row, col, half),) = units_of(PAIRS_C, h, z)
            table_c[own] = swap, 0, 1, half
            y, x, core = min(
                ((y, x, core) for y in (0, 1) for x in range(NX) for core in (0, 1)
                 if halves[(y * NX + x) * 2 + core, own] != half),
                key=lambda place: (min((place[1] - col // 2) % NX, (col // 2 - place[1]) % NX), place),
            )
            target_c[own] = (y, x, core)
            final[half].append((device(y, x, core, own), col * GROUPS + row))
            final_c[half].append((device(1 - y, x, core, own), col * GROUPS + row))
    return tables.reshape(2, 16 * GROUPS, 20), table_c, target_c, first, halves, final, final_c


def dot_t(a, b):
    return lax.dot_general(a, b, (((1,), (1,)), ((), ())), preferred_element_type=jnp.float32)


def half_product(rows, cols, half):
    at = pl.ds(pl.multiple_of(half * 256, 256), 256)
    total = dot_t(rows[0, at, :], cols[0])
    for k in range(1, rows.shape[0]):
        total += dot_t(rows[k, at, :], cols[k])
    return total


def units_kernel(pairs, index_pairs, spare, table, *refs):
    held, outs = refs[: len(refs) - spare], refs[len(refs) - spare :]
    for at, ((first, second), (_, _, halves)) in enumerate(zip(index_pairs, pairs)):
        swap, one, two, half = (table[4 * at + i] for i in range(4))
        for turned in range(1 if first == second else 2):
            rows, cols = (held[second], held[first]) if turned else (held[first], held[second])
            if halves is both:

                @pl.when(swap == turned)
                def _():
                    outs[1][two] = half_product(rows, cols, 1 - half)
                    outs[0][one] = half_product(rows, cols, half)

            else:
                for mine in range(2 - len(outs), 2):

                    @pl.when((swap == turned) & (two == mine))
                    def _():
                        outs[1 - mine][one] = half_product(rows, cols, half)


def products(table, held, names, pairs, counts):
    index_pairs = tuple((names.index(a), names.index(b)) for a, b, _ in pairs)
    return pl.pallas_call(
        functools.partial(units_kernel, pairs, index_pairs, len(counts)),
        out_shape=[pltpu.VMEM((count, 256, 512), jnp.float32) for count in counts],
        in_specs=[pl.BlockSpec(memory_space=pltpu.SMEM)]
        + [pl.BlockSpec(memory_space=pltpu.VMEM)] * len(held),
        out_specs=[pl.BlockSpec(memory_space=pltpu.VMEM)] * len(counts),
        compiler_params=pltpu.CompilerParams(vmem_limit_bytes=VMEM_LIMIT),
    )(table, *held)


def toward(targets, source, only):
    return [
        (device(*source(y, x, c, step), b), device(*only(y, x, c, step), b))
        for b, (y, x, c) in targets.items()
        for step in range(8)
    ]


def copy_kernel(source, out):
    out[...] = source[...]


def placed(value):
    return pl.pallas_call(
        copy_kernel,
        out_shape=pltpu.VMEM(value.shape, value.dtype),
        in_specs=[pl.BlockSpec(memory_space=pltpu.VMEM)],
        out_specs=pl.BlockSpec(memory_space=pltpu.VMEM),
        compiler_params=pltpu.CompilerParams(vmem_limit_bytes=VMEM_LIMIT),
    )(value)


def one_core(value, targets):
    def at(core_of):
        return lambda y, x, c, step: (step // NX, x + step % NX, core_of(c))

    return value + send(value, toward(targets, at(lambda c: 1 - c), at(lambda c: c)))


def along(targets, offset_from, offset_to):
    def at(offset):
        return lambda y, x, c, step: (step % 2, x + offset, c)

    return sorted(set(toward(targets, at(offset_from), at(offset_to))))


def one_x(value, targets):
    parts = [send(value, along(targets, offset, 0)) for offset in (2, 1, 3)]
    return value + parts[0] + (parts[1] + parts[2])


Y_SWAP = every(lambda y, x, c, h, z: (1 - y, x, c, block(h, z)))
CORE_SWAP = every(lambda y, x, c, h, z: (y, x, 1 - c, block(h, z)))
FROM_LEFT = every(lambda y, x, c, h, z: (y, x - 1, c, block(h, z)))
FROM_FAR = every(lambda y, x, c, h, z: (y, x + 2, c, block(h, z)))
FROM_RIGHT = every(lambda y, x, c, h, z: (y, x + 1, c, block(h, z)))
FROM_UP = every(lambda y, x, c, h, z: (y, x, c, block(h, z + 1)))
FROM_DOWN = every(lambda y, x, c, h, z: (y, x, c, block(h, z - 1)))
FROM_OTHER = every(lambda y, x, c, h, z: (y, x, c, block(h + 1, z)))


def near(keep, got):
    middle = keep.shape[1] // 2
    far_top = send(keep[2, :middle] + got[2, :middle], FROM_LEFT)
    far_bottom = send(keep[2, middle:] + got[2, middle:], FROM_RIGHT)
    right = keep[1] + got[1]
    right = jnp.concatenate([right[:middle] + far_top, right[middle:]], 0)
    left = keep[3] + got[3]
    left = jnp.concatenate([left[:middle], left[middle:] + far_bottom], 0)
    return keep[0] + got[0], right, left


def together(*values):
    return lax.optimization_barrier(values)


def over_x(keep, got):
    own, *others = together(*(keep[j] + got[j] for j in range(NX)))
    right, far, left = (send(part, pairs) for part, pairs in zip(others, (FROM_LEFT, FROM_FAR, FROM_RIGHT)))
    return own + far + (right + left)


def per_device(half_b):
    local, codes_c, target_c, first, halves, final, final_c = plan()
    aux, blk = lax.axis_index("aux"), lax.axis_index("blk")
    place = aux * GROUPS + blk
    table_a, table_b = jnp.asarray(local[0])[place], jnp.asarray(local[1])[place]
    table_c = jnp.asarray(codes_c)[blk]

    held = {O: placed(half_b)}
    held[PZ] = send(half_b, FROM_UP)
    held[MZ] = send(half_b, FROM_DOWN)
    held[Y0] = send(half_b, FROM_OTHER)
    held[O], held[PZ], held[MZ], held[Y0] = together(held[O], held[PZ], held[MZ], held[Y0])

    held[PP] = send(held[PZ], FROM_UP)
    held[MM] = send(held[MZ], FROM_DOWN)
    held[Y1] = send(held[PZ], FROM_OTHER)
    keep, given = products(table_a, [held[n] for n in HELD_A], HELD_A, PAIRS_A, (NX, NX))
    own_a, right_a, left_a = near(keep, send(given, CORE_SWAP))
    total_a = own_a + send(right_a, FROM_LEFT) + send(left_a, FROM_RIGHT)
    total_a, held[PP], held[MM], held[Y1] = together(total_a, held[PP], held[MM], held[Y1])

    held[Y2] = send(held[PP], FROM_OTHER)
    keep, given = products(table_b, [held[n] for n in HELD_B], HELD_B, PAIRS_B, (NX, NX))
    total_b = over_x(keep, send(given, CORE_SWAP))
    total_b, held[Y2] = together(total_b, held[Y2])

    has_first = jnp.asarray(first)[aux, blk]
    done = jnp.where(has_first, total_a, total_b) + send(jnp.where(has_first, total_b, total_a), Y_SWAP)
    (part_c,) = products(table_c, [held[n] for n in HELD_C], HELD_C, PAIRS_C, (1,))
    part_c = one_x(one_core(part_c[0], target_c), target_c)
    done, part_c = together(done, part_c)

    own_half = jnp.asarray(halves)[aux, blk]
    top = send(jnp.where(own_half == 0, done, part_c), final[0]) + send(part_c, final_c[0])
    bottom = send(jnp.where(own_half == 1, done, part_c), final[1]) + send(part_c, final_c[1])
    return jnp.concatenate([top, bottom], 0)


def solution(mesh):
    placed = (P("aux", "blk", None),)
    return jax.shard_map(
        per_device, mesh=mesh, in_specs=placed, out_specs=P("blk", "aux"), check_vma=False
    )
```

```python
import collections
import functools
import random

import jax
import jax.numpy as jnp
import numpy as np
from jax import lax
from jax.experimental import pallas as pl
from jax.experimental.pallas import tpu as pltpu
from jax.sharding import PartitionSpec as P

ALL = ("aux", "blk")
NX, NZ, GROUPS = 4, 8, 16
VMEM_LIMIT = 16 * 2**20


def device(y_lo, x, core, blk):
    return ((y_lo * NX + x % NX) * 2 + core) * GROUPS + blk


def block(h, z):
    return h % 2 * NZ + z % NZ


def every(move):
    return [
        (device(*move(y_lo, x, core, h, z)), device(y_lo, x, core, block(h, z)))
        for y_lo in range(2)
        for x in range(NX)
        for core in range(2)
        for h in range(2)
        for z in range(NZ)
    ]


def send(value, pairs):
    return lax.ppermute(value, ALL, pairs)


O, PZ, MZ, Y0 = (0, 0), (0, 1), (0, -1), (1, 0)
PP, MM, Y1, Y2 = (0, 2), (0, -2), (1, 1), (1, 2)
HELD_A = (O, PZ, MZ, Y0)
HELD_B = (O, MZ, PP, MM, Y1)
HELD_C = (MM, Y2)


def units_of(pairs, h, z):
    found = []
    for at, (first, second, halves) in enumerate(pairs):
        i, j = block(h + first[0], z + first[1]), block(h + second[0], z + second[1])
        for half in halves(h, z):
            core = half if halves is both else int(first == second)
            found.append(((at, int(i > j), core), min(i, j), max(i, j), half))
    return found


def both(h, z):
    return (0, 1)


def by_h(h, z):
    return (h,)


def by_z(h, z):
    return (0,) if 2 <= z < 6 else (1,)


def upper(h, z):
    return (0,)


def lower(h, z):
    return (1,)


PAIRS_A = ((O, PZ, both), (MZ, PZ, both), (O, Y0, by_h), (MZ, Y0, both), (O, O, upper))
PAIRS_B = ((MZ, PP, both), (MM, PP, by_z), (MZ, Y1, both), (MM, Y1, both), (O, O, lower))
PAIRS_C = ((MM, Y2, by_h),)


def steps(a, b, n):
    ahead, back = (b - a) % n, (a - b) % n
    found = []
    if ahead and ahead <= back:
        found += [((a + i) % n, 1, 1.0) for i in range(ahead)]
    if ahead and back <= ahead:
        found += [((a - i) % n, -1, 1.0) for i in range(back)]
    return found


@functools.cache
def route(source, target):
    found = []
    for weight, order in ((1.0, (2, 0, 1)), (0.01, (2, 1, 0))):
        at = list(source)
        for axis in order:
            for place, way, share in steps(at[axis], target[axis], (NX, 4, NZ)[axis]):
                link = at[:axis] + [place] + at[axis + 1 :]
                found.append(((weight, axis, way, *link), share))
            at[axis] = target[axis]
    return found


def links(own, place, y, unit):
    h, z = own // NZ, own % NZ
    _, row, col, _ = unit
    return route((place // 2, 2 * h + y, z), (col // 2 % NX, row // NZ * 2 + col // NZ, row % NZ))


def by_core(units):
    cores = [[index for index, unit in enumerate(units) if unit[0][2] == core] for core in (0, 1)]
    return [cores[place % 2][place // 2] for place in range(8)]


@functools.cache
def spread(trials=120000):
    draw = random.Random(0)
    where = [(own // NZ, own % NZ) for own in range(GROUPS)]
    units = [[units_of(pairs, h, z) for pairs in (PAIRS_A, PAIRS_B)] for h, z in where]
    at = [[by_core(batch) for batch in both_batches] for both_batches in units]
    planes = [[h] * 8 for h, _ in where]
    load = collections.Counter()

    def on(own, batch, place, index, y):
        return links(own, place, 1 - y if batch else y, units[own][batch][index])

    for own, (h, z) in enumerate(where):
        for batch in (0, 1):
            for place in range(8):
                for link, share in on(own, batch, place, at[own][batch][place], planes[own][place]):
                    load[link] += share
        for unit in units_of(PAIRS_C, h, z):
            for y in (0, 1):
                for link, share in links(own, unit[2] % 8, y, unit):
                    load[link] += share
    for _ in range(trials):
        own, batch, u, v = draw.randrange(GROUPS), draw.randrange(2), draw.randrange(8), draw.randrange(8)
        if (u - v) % 2:
            continue
        now, plane = at[own], planes[own]
        change = collections.Counter()
        if u == v:
            for one in (0, 1):
                for sign, y in ((-1, plane[u]), (1, 1 - plane[u])):
                    for link, share in on(own, one, u, now[one][u], y):
                        change[link] += sign * share
        else:
            i, j = now[batch][u], now[batch][v]
            for sign, place, index in ((-1, u, i), (-1, v, j), (1, u, j), (1, v, i)):
                for link, share in on(own, batch, place, index, plane[place]):
                    change[link] += sign * share
        if sum(link[0] * ((load[link] + d) ** 6 - load[link] ** 6) for link, d in change.items()) <= 0:
            for link, d in change.items():
                load[link] += d
            if u == v:
                plane[u] = 1 - plane[u]
            else:
                now[batch][u], now[batch][v] = j, i
    return units, at, planes


@functools.cache
def plan():
    tables = np.zeros((2, 16, GROUPS, 5, 4), np.int32)
    table_c = np.zeros((GROUPS, 4), np.int32)
    target_c = {}
    final = {half: [] for half in (0, 1)}
    final_c = {half: [] for half in (0, 1)}
    halves = np.zeros((16, GROUPS), np.int32)
    first = np.zeros((16, GROUPS), np.bool_)
    units, at, planes = spread()
    for h in range(2):
        for z in range(NZ):
            own = block(h, z)
            for place in range(8):
                x, core = place // 2, place % 2
                for batch in range(2):
                    (pair, swap, _), row, col, half = units[own][batch][at[own][batch][place]]
                    y = 1 - planes[own][place] if batch else planes[own][place]
                    final[half].append((device(y, x, core, own), col * GROUPS + row))
                    first[(y * NX + x) * 2 + core, own] = not batch
                    halves[(y * NX + x) * 2 + core, own] = half
                    for aux in range(16):
                        entry, offset = tables[batch, aux, own, pair], (x - aux // 2) % NX
                        kept = aux % 2 == core
                        entry[0] = swap
                        if (PAIRS_A, PAIRS_B)[batch][pair][2] is both:
                            entry[1 if kept else 2] = offset
                            entry[3] = aux % 2
                        else:
                            entry[1:] = offset, kept, half
            (((_, swap, _), row, col, half),) = units_of(PAIRS_C, h, z)
            table_c[own] = swap, 0, 1, half
            y, x, core = min(
                ((y, x, core) for y in (0, 1) for x in range(NX) for core in (0, 1)
                 if halves[(y * NX + x) * 2 + core, own] != half),
                key=lambda place: (min((place[1] - col // 2) % NX, (col // 2 - place[1]) % NX), place),
            )
            target_c[own] = (y, x, core)
            final[half].append((device(y, x, core, own), col * GROUPS + row))
            final_c[half].append((device(1 - y, x, core, own), col * GROUPS + row))
    return tables.reshape(2, 16 * GROUPS, 20), table_c, target_c, first, halves, final, final_c


def dot_t(a, b):
    return lax.dot_general(a, b, (((1,), (1,)), ((), ())), preferred_element_type=jnp.float32)


def half_product(rows, cols, half):
    at = pl.ds(pl.multiple_of(half * 256, 256), 256)
    total = dot_t(rows[0, at, :], cols[0])
    for k in range(1, rows.shape[0]):
        total += dot_t(rows[k, at, :], cols[k])
    return total


def units_kernel(pairs, index_pairs, spare, table, *refs):
    held, outs = refs[: len(refs) - spare], refs[len(refs) - spare :]
    for at, ((first, second), (_, _, halves)) in enumerate(zip(index_pairs, pairs)):
        swap, one, two, half = (table[4 * at + i] for i in range(4))
        for turned in range(1 if first == second else 2):
            rows, cols = (held[second], held[first]) if turned else (held[first], held[second])
            if halves is both:

                @pl.when(swap == turned)
                def _():
                    outs[1][two] = half_product(rows, cols, 1 - half)
                    outs[0][one] = half_product(rows, cols, half)

            else:
                for mine in range(2 - len(outs), 2):

                    @pl.when((swap == turned) & (two == mine))
                    def _():
                        outs[1 - mine][one] = half_product(rows, cols, half)


def products(table, held, names, pairs, counts):
    index_pairs = tuple((names.index(a), names.index(b)) for a, b, _ in pairs)
    return pl.pallas_call(
        functools.partial(units_kernel, pairs, index_pairs, len(counts)),
        out_shape=[pltpu.VMEM((count, 256, 512), jnp.float32) for count in counts],
        in_specs=[pl.BlockSpec(memory_space=pltpu.SMEM)]
        + [pl.BlockSpec(memory_space=pltpu.VMEM)] * len(held),
        out_specs=[pl.BlockSpec(memory_space=pltpu.VMEM)] * len(counts),
        compiler_params=pltpu.CompilerParams(vmem_limit_bytes=VMEM_LIMIT),
    )(table, *held)


def toward(targets, source, only):
    return [
        (device(*source(y, x, c, step), b), device(*only(y, x, c, step), b))
        for b, (y, x, c) in targets.items()
        for step in range(8)
    ]


def copy_kernel(source, out):
    out[...] = source[...]


def placed(value):
    return pl.pallas_call(
        copy_kernel,
        out_shape=pltpu.VMEM(value.shape, value.dtype),
        in_specs=[pl.BlockSpec(memory_space=pltpu.VMEM)],
        out_specs=pl.BlockSpec(memory_space=pltpu.VMEM),
        compiler_params=pltpu.CompilerParams(vmem_limit_bytes=VMEM_LIMIT),
    )(value)


def one_core(value, targets):
    def at(core_of):
        return lambda y, x, c, step: (step // NX, x + step % NX, core_of(c))

    return value + send(value, toward(targets, at(lambda c: 1 - c), at(lambda c: c)))


def along(targets, offset_from, offset_to):
    def at(offset):
        return lambda y, x, c, step: (step % 2, x + offset, c)

    return sorted(set(toward(targets, at(offset_from), at(offset_to))))


def one_x(value, targets):
    parts = [send(value, along(targets, offset, 0)) for offset in (2, 1, 3)]
    return value + parts[0] + (parts[1] + parts[2])


Y_SWAP = every(lambda y, x, c, h, z: (1 - y, x, c, block(h, z)))
CORE_SWAP = every(lambda y, x, c, h, z: (y, x, 1 - c, block(h, z)))
FROM_LEFT = every(lambda y, x, c, h, z: (y, x - 1, c, block(h, z)))
FROM_FAR = every(lambda y, x, c, h, z: (y, x + 2, c, block(h, z)))
FROM_RIGHT = every(lambda y, x, c, h, z: (y, x + 1, c, block(h, z)))
FROM_UP = every(lambda y, x, c, h, z: (y, x, c, block(h, z + 1)))
FROM_DOWN = every(lambda y, x, c, h, z: (y, x, c, block(h, z - 1)))
FROM_OTHER = every(lambda y, x, c, h, z: (y, x, c, block(h + 1, z)))


def near(keep, got):
    middle = keep.shape[1] // 2
    far_top = send(keep[2, :middle] + got[2, :middle], FROM_LEFT)
    far_bottom = send(keep[2, middle:] + got[2, middle:], FROM_RIGHT)
    right = keep[1] + got[1]
    right = jnp.concatenate([right[:middle] + far_top, right[middle:]], 0)
    left = keep[3] + got[3]
    left = jnp.concatenate([left[:middle], left[middle:] + far_bottom], 0)
    return keep[0] + got[0], right, left


def split(value):
    return [value[j] for j in range(NX)]


def together(*values):
    return lax.optimization_barrier(values)


def per_device(half_b):
    local, codes_c, target_c, first, halves, final, final_c = plan()
    aux, blk = lax.axis_index("aux"), lax.axis_index("blk")
    place = aux * GROUPS + blk
    table_a, table_b = jnp.asarray(local[0])[place], jnp.asarray(local[1])[place]
    table_c = jnp.asarray(codes_c)[blk]

    held = {O: placed(half_b)}
    held[PZ] = send(half_b, FROM_UP)
    held[MZ] = send(half_b, FROM_DOWN)
    held[Y0] = send(half_b, FROM_OTHER)
    held[O], held[PZ], held[MZ], held[Y0] = together(held[O], held[PZ], held[MZ], held[Y0])

    held[PP] = send(held[PZ], FROM_UP)
    held[MM] = send(held[MZ], FROM_DOWN)
    held[Y1] = send(held[PZ], FROM_OTHER)
    keep, given = products(table_a, [held[n] for n in HELD_A], HELD_A, PAIRS_A, (NX, NX))
    own_a, right_a, left_a = near(keep, send(given, CORE_SWAP))
    total_a = own_a + send(right_a, FROM_LEFT) + send(left_a, FROM_RIGHT)
    total_a, held[PP], held[MM], held[Y1] = together(total_a, held[PP], held[MM], held[Y1])

    held[Y2] = send(held[PP], FROM_OTHER)
    keep, given = products(table_b, [held[n] for n in HELD_B], HELD_B, PAIRS_B, (NX, NX))
    own, *others = together(*(k + g for k, g in zip(split(keep), split(send(given, CORE_SWAP)))))
    right, far, left = (send(part, pairs) for part, pairs in zip(others, (FROM_LEFT, FROM_FAR, FROM_RIGHT)))
    held[Y2], right = together(held[Y2], right)
    (part_c,) = products(table_c, [held[n] for n in HELD_C], HELD_C, PAIRS_C, (1,))
    part_c = one_core(part_c[0], target_c)
    total_b, part_c = together((own + right) + (far + left), part_c)

    has_first = jnp.asarray(first)[aux, blk]
    done = jnp.where(has_first, total_a, total_b) + send(jnp.where(has_first, total_b, total_a), Y_SWAP)
    part_c = one_x(part_c, target_c)
    done, part_c = together(done, part_c)

    own_half = jnp.asarray(halves)[aux, blk]
    top = send(jnp.where(own_half == 0, done, part_c), final[0]) + send(part_c, final_c[0])
    bottom = send(jnp.where(own_half == 1, done, part_c), final[1]) + send(part_c, final_c[1])
    return jnp.concatenate([top, bottom], 0)


def solution(mesh):
    placed = (P("aux", "blk", None),)
    return jax.shard_map(
        per_device, mesh=mesh, in_specs=placed, out_specs=P("blk", "aux"), check_vma=False
    )
```

```python
import collections
import functools
import random

import jax
import jax.numpy as jnp
import numpy as np
from jax import lax
from jax.experimental import pallas as pl
from jax.experimental.pallas import tpu as pltpu
from jax.sharding import PartitionSpec as P

ALL = ("aux", "blk")
NX, NZ, GROUPS = 4, 8, 16
VMEM_LIMIT = 16 * 2**20


def device(y_lo, x, core, blk):
    return ((y_lo * NX + x % NX) * 2 + core) * GROUPS + blk


def block(h, z):
    return h % 2 * NZ + z % NZ


def every(move):
    return [
        (device(*move(y_lo, x, core, h, z)), device(y_lo, x, core, block(h, z)))
        for y_lo in range(2)
        for x in range(NX)
        for core in range(2)
        for h in range(2)
        for z in range(NZ)
    ]


def send(value, pairs):
    return lax.ppermute(value, ALL, pairs)


O, PZ, MZ, Y0 = (0, 0), (0, 1), (0, -1), (1, 0)
PP, MM, Y1, Y2 = (0, 2), (0, -2), (1, 1), (1, 2)
HELD_A = (O, PZ, MZ, Y0)
HELD_B = (O, MZ, PP, MM, Y1)
HELD_C = (MM, Y2)


def units_of(pairs, h, z):
    found = []
    for at, (first, second, halves) in enumerate(pairs):
        i, j = block(h + first[0], z + first[1]), block(h + second[0], z + second[1])
        for half in halves(h, z):
            core = half if halves is both else int(first == second)
            found.append(((at, int(i > j), core), min(i, j), max(i, j), half))
    return found


def both(h, z):
    return (0, 1)


def by_h(h, z):
    return (h,)


def by_z(h, z):
    return (0,) if 2 <= z < 6 else (1,)


def upper(h, z):
    return (0,)


def lower(h, z):
    return (1,)


PAIRS_A = ((O, PZ, both), (MZ, PZ, both), (O, Y0, by_h), (MZ, Y0, both), (O, O, upper))
PAIRS_B = ((MZ, PP, both), (MM, PP, by_z), (MZ, Y1, both), (MM, Y1, both), (O, O, lower))
PAIRS_C = ((MM, Y2, by_h),)


def steps(a, b, n):
    ahead, back = (b - a) % n, (a - b) % n
    found = []
    if ahead and ahead <= back:
        found += [((a + i) % n, 1, 1.0) for i in range(ahead)]
    if ahead and back <= ahead:
        found += [((a - i) % n, -1, 1.0) for i in range(back)]
    return found


@functools.cache
def route(source, target):
    found = []
    for weight, order in ((1.0, (2, 0, 1)), (0.01, (2, 1, 0))):
        at = list(source)
        for axis in order:
            for place, way, share in steps(at[axis], target[axis], (NX, 4, NZ)[axis]):
                link = at[:axis] + [place] + at[axis + 1 :]
                found.append(((weight, axis, way, *link), share))
            at[axis] = target[axis]
    return found


def links(own, place, y, unit):
    h, z = own // NZ, own % NZ
    _, row, col, _ = unit
    return route((place // 2, 2 * h + y, z), (col // 2 % NX, row // NZ * 2 + col // NZ, row % NZ))


def by_core(units):
    cores = [[index for index, unit in enumerate(units) if unit[0][2] == core] for core in (0, 1)]
    return [cores[place % 2][place // 2] for place in range(8)]


@functools.cache
def spread(trials=120000):
    draw = random.Random(0)
    where = [(own // NZ, own % NZ) for own in range(GROUPS)]
    units = [[units_of(pairs, h, z) for pairs in (PAIRS_A, PAIRS_B)] for h, z in where]
    at = [[by_core(batch) for batch in both_batches] for both_batches in units]
    planes = [[h] * 8 for h, _ in where]
    load = collections.Counter()

    def on(own, batch, place, index, y):
        return links(own, place, 1 - y if batch else y, units[own][batch][index])

    for own, (h, z) in enumerate(where):
        for batch in (0, 1):
            for place in range(8):
                for link, share in on(own, batch, place, at[own][batch][place], planes[own][place]):
                    load[link] += share
        for unit in units_of(PAIRS_C, h, z):
            for link, share in links(own, unit[2] % 8, 1 - h, unit):
                load[link] += share
    for _ in range(trials):
        own, batch, u, v = draw.randrange(GROUPS), draw.randrange(2), draw.randrange(8), draw.randrange(8)
        if (u - v) % 2:
            continue
        now, plane = at[own], planes[own]
        change = collections.Counter()
        if u == v:
            for one in (0, 1):
                for sign, y in ((-1, plane[u]), (1, 1 - plane[u])):
                    for link, share in on(own, one, u, now[one][u], y):
                        change[link] += sign * share
        else:
            i, j = now[batch][u], now[batch][v]
            for sign, place, index in ((-1, u, i), (-1, v, j), (1, u, j), (1, v, i)):
                for link, share in on(own, batch, place, index, plane[place]):
                    change[link] += sign * share
        if sum(link[0] * ((load[link] + d) ** 6 - load[link] ** 6) for link, d in change.items()) <= 0:
            for link, d in change.items():
                load[link] += d
            if u == v:
                plane[u] = 1 - plane[u]
            else:
                now[batch][u], now[batch][v] = j, i
    return units, at, planes


@functools.cache
def plan():
    tables = np.zeros((2, 16, GROUPS, 5, 4), np.int32)
    table_c = np.zeros((GROUPS, 4), np.int32)
    target_c = {}
    final = {half: [] for half in (0, 1)}
    halves = np.zeros((16, GROUPS), np.int32)
    first = np.zeros((16, GROUPS), np.bool_)
    units, at, planes = spread()
    for h in range(2):
        for z in range(NZ):
            own = block(h, z)
            for place in range(8):
                x, core = place // 2, place % 2
                for batch in range(2):
                    (pair, swap, _), row, col, half = units[own][batch][at[own][batch][place]]
                    y = 1 - planes[own][place] if batch else planes[own][place]
                    final[half].append((device(y, x, core, own), col * GROUPS + row))
                    first[(y * NX + x) * 2 + core, own] = not batch
                    halves[(y * NX + x) * 2 + core, own] = half
                    for aux in range(16):
                        entry, offset = tables[batch, aux, own, pair], (x - aux // 2) % NX
                        kept = aux % 2 == core
                        entry[0] = swap
                        if (PAIRS_A, PAIRS_B)[batch][pair][2] is both:
                            entry[1 if kept else 2] = offset
                            entry[3] = aux % 2
                        else:
                            entry[1:] = offset, kept, half
            (((_, swap, _), row, col, half),) = units_of(PAIRS_C, h, z)
            table_c[own] = swap, 0, 1, half
            y, x, core = min(
                ((y, x, core) for y in (0, 1) for x in range(NX) for core in (0, 1)
                 if halves[(y * NX + x) * 2 + core, own] != half),
                key=lambda place: (min((place[1] - col // 2) % NX, (col // 2 - place[1]) % NX), place),
            )
            target_c[own] = (y, x, core)
            final[half].append((device(y, x, core, own), col * GROUPS + row))
    return tables.reshape(2, 16 * GROUPS, 20), table_c, target_c, first, halves, final


def dot_t(a, b):
    return lax.dot_general(a, b, (((1,), (1,)), ((), ())), preferred_element_type=jnp.float32)


def half_product(rows, cols, half):
    at = pl.ds(pl.multiple_of(half * 256, 256), 256)
    total = dot_t(rows[0, at, :], cols[0])
    for k in range(1, rows.shape[0]):
        total += dot_t(rows[k, at, :], cols[k])
    return total


def units_kernel(pairs, index_pairs, spare, table, *refs):
    held, outs = refs[: len(refs) - spare], refs[len(refs) - spare :]
    for at, ((first, second), (_, _, halves)) in enumerate(zip(index_pairs, pairs)):
        swap, one, two, half = (table[4 * at + i] for i in range(4))
        for turned in range(1 if first == second else 2):
            rows, cols = (held[second], held[first]) if turned else (held[first], held[second])
            if halves is both:

                @pl.when(swap == turned)
                def _():
                    outs[1][two] = half_product(rows, cols, 1 - half)
                    outs[0][one] = half_product(rows, cols, half)

            else:
                for mine in range(2 - len(outs), 2):

                    @pl.when((swap == turned) & (two == mine))
                    def _():
                        outs[1 - mine][one] = half_product(rows, cols, half)


def products(table, held, names, pairs, counts):
    index_pairs = tuple((names.index(a), names.index(b)) for a, b, _ in pairs)
    return pl.pallas_call(
        functools.partial(units_kernel, pairs, index_pairs, len(counts)),
        out_shape=[pltpu.VMEM((count, 256, 512), jnp.float32) for count in counts],
        in_specs=[pl.BlockSpec(memory_space=pltpu.SMEM)]
        + [pl.BlockSpec(memory_space=pltpu.VMEM)] * len(held),
        out_specs=[pl.BlockSpec(memory_space=pltpu.VMEM)] * len(counts),
        compiler_params=pltpu.CompilerParams(vmem_limit_bytes=VMEM_LIMIT),
    )(table, *held)


def toward(targets, source, only):
    return [
        (device(*source(y, x, c, step), b), device(*only(y, x, c, step), b))
        for b, (y, x, c) in targets.items()
        for step in range(8)
    ]


def copy_kernel(source, out):
    out[...] = source[...]


def placed(value):
    return pl.pallas_call(
        copy_kernel,
        out_shape=pltpu.VMEM(value.shape, value.dtype),
        in_specs=[pl.BlockSpec(memory_space=pltpu.VMEM)],
        out_specs=pl.BlockSpec(memory_space=pltpu.VMEM),
        compiler_params=pltpu.CompilerParams(vmem_limit_bytes=VMEM_LIMIT),
    )(value)


def one_core(value, targets):
    def at(core_of):
        return lambda y, x, c, step: (step // NX, x + step % NX, core_of(c))

    return value + send(value, toward(targets, at(lambda c: 1 - c), at(lambda c: c)))


def along(targets, offset_from, offset_to):
    def at(offset):
        return lambda y, x, c, step: (step % 2, x + offset, c)

    return sorted(set(toward(targets, at(offset_from), at(offset_to))))


def one_x(value, targets):
    parts = [send(value, along(targets, offset, 0)) for offset in (2, 1, 3)]
    return value + parts[0] + (parts[1] + parts[2])


def one_y(value, targets):
    pairs = [(device(1 - y, x, c, b), device(y, x, c, b)) for b, (y, x, c) in targets.items()]
    return value + send(value, pairs)


Y_SWAP = every(lambda y, x, c, h, z: (1 - y, x, c, block(h, z)))
CORE_SWAP = every(lambda y, x, c, h, z: (y, x, 1 - c, block(h, z)))
FROM_LEFT = every(lambda y, x, c, h, z: (y, x - 1, c, block(h, z)))
FROM_FAR = every(lambda y, x, c, h, z: (y, x + 2, c, block(h, z)))
FROM_RIGHT = every(lambda y, x, c, h, z: (y, x + 1, c, block(h, z)))
FROM_UP = every(lambda y, x, c, h, z: (y, x, c, block(h, z + 1)))
FROM_DOWN = every(lambda y, x, c, h, z: (y, x, c, block(h, z - 1)))
FROM_OTHER = every(lambda y, x, c, h, z: (y, x, c, block(h + 1, z)))


def near(keep, got):
    middle = keep.shape[1] // 2
    far_top = send(keep[2, :middle] + got[2, :middle], FROM_LEFT)
    far_bottom = send(keep[2, middle:] + got[2, middle:], FROM_RIGHT)
    right = keep[1] + got[1]
    right = jnp.concatenate([right[:middle] + far_top, right[middle:]], 0)
    left = keep[3] + got[3]
    left = jnp.concatenate([left[:middle], left[middle:] + far_bottom], 0)
    return keep[0] + got[0], right, left


def split(value):
    return [value[j] for j in range(NX)]


def together(*values):
    return lax.optimization_barrier(values)


def per_device(half_b):
    local, codes_c, target_c, first, halves, final = plan()
    aux, blk = lax.axis_index("aux"), lax.axis_index("blk")
    place = aux * GROUPS + blk
    table_a, table_b = jnp.asarray(local[0])[place], jnp.asarray(local[1])[place]
    table_c = jnp.asarray(codes_c)[blk]

    held = {O: placed(half_b)}
    held[PZ] = send(half_b, FROM_UP)
    held[MZ] = send(half_b, FROM_DOWN)
    held[Y0] = send(half_b, FROM_OTHER)
    held[O], held[PZ], held[MZ], held[Y0] = together(held[O], held[PZ], held[MZ], held[Y0])

    held[PP] = send(held[PZ], FROM_UP)
    held[MM] = send(held[MZ], FROM_DOWN)
    held[Y1] = send(held[PZ], FROM_OTHER)
    keep, given = products(table_a, [held[n] for n in HELD_A], HELD_A, PAIRS_A, (NX, NX))
    own_a, right_a, left_a = near(keep, send(given, CORE_SWAP))
    total_a = own_a + send(right_a, FROM_LEFT) + send(left_a, FROM_RIGHT)
    total_a, held[PP], held[MM], held[Y1] = together(total_a, held[PP], held[MM], held[Y1])

    held[Y2] = send(held[PP], FROM_OTHER)
    keep, given = products(table_b, [held[n] for n in HELD_B], HELD_B, PAIRS_B, (NX, NX))
    own, *others = together(*(k + g for k, g in zip(split(keep), split(send(given, CORE_SWAP)))))
    right, far, left = (send(part, pairs) for part, pairs in zip(others, (FROM_LEFT, FROM_FAR, FROM_RIGHT)))
    held[Y2], right = together(held[Y2], right)
    (part_c,) = products(table_c, [held[n] for n in HELD_C], HELD_C, PAIRS_C, (1,))
    part_c = one_core(part_c[0], target_c)
    total_b, part_c = together((own + right) + (far + left), part_c)

    has_first = jnp.asarray(first)[aux, blk]
    done = jnp.where(has_first, total_a, total_b) + send(jnp.where(has_first, total_b, total_a), Y_SWAP)
    part_c = one_y(one_x(part_c, target_c), target_c)
    done, part_c = together(done, part_c)

    own_half = jnp.asarray(halves)[aux, blk]
    top = send(jnp.where(own_half == 0, done, part_c), final[0])
    bottom = send(jnp.where(own_half == 1, done, part_c), final[1])
    return jnp.concatenate([top, bottom], 0)


def solution(mesh):
    placed = (P("aux", "blk", None),)
    return jax.shard_map(
        per_device, mesh=mesh, in_specs=placed, out_specs=P("blk", "aux"), check_vma=False
    )
```

```python
import collections
import functools
import random

import jax
import jax.numpy as jnp
import numpy as np
from jax import lax
from jax.experimental import pallas as pl
from jax.experimental.pallas import tpu as pltpu
from jax.sharding import PartitionSpec as P

ALL = ("aux", "blk")
NX, NZ, GROUPS = 4, 8, 16
VMEM_LIMIT = 16 * 2**20


def device(y_lo, x, core, blk):
    return ((y_lo * NX + x % NX) * 2 + core) * GROUPS + blk


def block(h, z):
    return h % 2 * NZ + z % NZ


def every(move):
    return [
        (device(*move(y_lo, x, core, h, z)), device(y_lo, x, core, block(h, z)))
        for y_lo in range(2)
        for x in range(NX)
        for core in range(2)
        for h in range(2)
        for z in range(NZ)
    ]


def send(value, pairs):
    return lax.ppermute(value, ALL, pairs)


O, PZ, MZ, Y0 = (0, 0), (0, 1), (0, -1), (1, 0)
PP, MM, Y1, Y2 = (0, 2), (0, -2), (1, 1), (1, 2)
HELD_A = (O, PZ, MZ, Y0)
HELD_B = (O, MZ, PP, MM, Y1)
HELD_C = (MM, Y2)


def units_of(pairs, h, z):
    found = []
    for at, (first, second, halves) in enumerate(pairs):
        i, j = block(h + first[0], z + first[1]), block(h + second[0], z + second[1])
        for half in halves(h, z):
            core = half if halves is both else int(first == second)
            found.append(((at, int(i > j), core), min(i, j), max(i, j), half))
    return found


def both(h, z):
    return (0, 1)


def by_h(h, z):
    return (h,)


def by_z(h, z):
    return (0,) if 2 <= z < 6 else (1,)


def upper(h, z):
    return (0,)


def lower(h, z):
    return (1,)


PAIRS_A = ((O, PZ, both), (MZ, PZ, both), (O, Y0, by_h), (MZ, Y0, both), (O, O, upper))
PAIRS_B = ((MZ, PP, both), (MM, PP, by_z), (MZ, Y1, both), (MM, Y1, both), (O, O, lower))
PAIRS_C = ((MM, Y2, by_h),)


def steps(a, b, n):
    ahead, back = (b - a) % n, (a - b) % n
    found = []
    if ahead and ahead <= back:
        found += [((a + i) % n, 1, 1.0) for i in range(ahead)]
    if ahead and back <= ahead:
        found += [((a - i) % n, -1, 1.0) for i in range(back)]
    return found


@functools.cache
def route(source, target):
    found = []
    for weight, order in ((1.0, (2, 0, 1)), (0.01, (2, 1, 0))):
        at = list(source)
        for axis in order:
            for place, way, share in steps(at[axis], target[axis], (NX, 4, NZ)[axis]):
                link = at[:axis] + [place] + at[axis + 1 :]
                found.append(((weight, axis, way, *link), share))
            at[axis] = target[axis]
    return found


def links(own, place, y, unit):
    h, z = own // NZ, own % NZ
    _, row, col, _ = unit
    return route((place // 2, 2 * h + y, z), (col // 2 % NX, row // NZ * 2 + col // NZ, row % NZ))


def by_core(units):
    cores = [[index for index, unit in enumerate(units) if unit[0][2] == core] for core in (0, 1)]
    return [cores[place % 2][place // 2] for place in range(8)]


@functools.cache
def spread(trials=120000):
    draw = random.Random(0)
    where = [(own // NZ, own % NZ) for own in range(GROUPS)]
    units = [[units_of(pairs, h, z) for pairs in (PAIRS_A, PAIRS_B)] for h, z in where]
    at = [[by_core(batch) for batch in both_batches] for both_batches in units]
    planes = [[h] * 8 for h, _ in where]
    load = collections.Counter()

    def on(own, batch, place, index, y):
        return links(own, place, 1 - y if batch else y, units[own][batch][index])

    for own, (h, z) in enumerate(where):
        for batch in (0, 1):
            for place in range(8):
                for link, share in on(own, batch, place, at[own][batch][place], planes[own][place]):
                    load[link] += share
        for unit in units_of(PAIRS_C, h, z):
            for y in (0, 1):
                for link, share in links(own, unit[2] % 8, y, unit):
                    load[link] += share
    for _ in range(trials):
        own, batch, u, v = draw.randrange(GROUPS), draw.randrange(2), draw.randrange(8), draw.randrange(8)
        if (u - v) % 2:
            continue
        now, plane = at[own], planes[own]
        change = collections.Counter()
        if u == v:
            for one in (0, 1):
                for sign, y in ((-1, plane[u]), (1, 1 - plane[u])):
                    for link, share in on(own, one, u, now[one][u], y):
                        change[link] += sign * share
        else:
            i, j = now[batch][u], now[batch][v]
            for sign, place, index in ((-1, u, i), (-1, v, j), (1, u, j), (1, v, i)):
                for link, share in on(own, batch, place, index, plane[place]):
                    change[link] += sign * share
        if sum(link[0] * ((load[link] + d) ** 6 - load[link] ** 6) for link, d in change.items()) <= 0:
            for link, d in change.items():
                load[link] += d
            if u == v:
                plane[u] = 1 - plane[u]
            else:
                now[batch][u], now[batch][v] = j, i
    return units, at, planes


@functools.cache
def plan():
    tables = np.zeros((2, 16, GROUPS, 5, 4), np.int32)
    table_c = np.zeros((GROUPS, 4), np.int32)
    target_c = {}
    final = {half: [] for half in (0, 1)}
    final_c = {half: [] for half in (0, 1)}
    halves = np.zeros((16, GROUPS), np.int32)
    first = np.zeros((16, GROUPS), np.bool_)
    units, at, planes = spread()
    for h in range(2):
        for z in range(NZ):
            own = block(h, z)
            for place in range(8):
                x, core = place // 2, place % 2
                for batch in range(2):
                    (pair, swap, _), row, col, half = units[own][batch][at[own][batch][place]]
                    y = 1 - planes[own][place] if batch else planes[own][place]
                    final[half].append((device(y, x, core, own), col * GROUPS + row))
                    first[(y * NX + x) * 2 + core, own] = not batch
                    halves[(y * NX + x) * 2 + core, own] = half
                    for aux in range(16):
                        entry, offset = tables[batch, aux, own, pair], (x - aux // 2) % NX
                        kept = aux % 2 == core
                        entry[0] = swap
                        if (PAIRS_A, PAIRS_B)[batch][pair][2] is both:
                            entry[1 if kept else 2] = offset
                            entry[3] = aux % 2
                        else:
                            entry[1:] = offset, kept, half
            (((_, swap, _), row, col, half),) = units_of(PAIRS_C, h, z)
            table_c[own] = swap, 0, 1, half
            y, x, core = min(
                ((y, x, core) for y in (0, 1) for x in range(NX) for core in (0, 1)
                 if halves[(y * NX + x) * 2 + core, own] != half),
                key=lambda place: (min((place[1] - col // 2) % NX, (col // 2 - place[1]) % NX), place),
            )
            target_c[own] = (y, x, core)
            final[half].append((device(y, x, core, own), col * GROUPS + row))
            final_c[half].append((device(1 - y, x, core, own), col * GROUPS + row))
    return tables.reshape(2, 16 * GROUPS, 20), table_c, target_c, first, halves, final, final_c


def dot_t(a, b):
    return lax.dot_general(a, b, (((1,), (1,)), ((), ())), preferred_element_type=jnp.float32)


def half_product(rows, cols, half):
    at = pl.ds(pl.multiple_of(half * 256, 256), 256)
    total = dot_t(rows[0, at, :], cols[0])
    for k in range(1, rows.shape[0]):
        total += dot_t(rows[k, at, :], cols[k])
    return total


def units_kernel(pairs, index_pairs, kept, table, *refs):
    held, out = refs[:-1], refs[-1]
    for at, ((first, second), (_, _, halves)) in enumerate(zip(index_pairs, pairs)):
        swap, one, two, half = (table[4 * at + i] for i in range(4))
        for turned in range(1 if first == second else 2):
            rows, cols = (held[second], held[first]) if turned else (held[first], held[second])
            if halves is both:

                @pl.when(swap == turned)
                def _():
                    out[one if kept else two] = half_product(rows, cols, half if kept else 1 - half)

            else:

                @pl.when((swap == turned) & (two == kept))
                def _():
                    out[one] = half_product(rows, cols, half)


def products(table, held, names, pairs, kept, count=NX):
    index_pairs = tuple((names.index(a), names.index(b)) for a, b, _ in pairs)
    return pl.pallas_call(
        functools.partial(units_kernel, pairs, index_pairs, kept),
        out_shape=pltpu.VMEM((count, 256, 512), jnp.float32),
        in_specs=[pl.BlockSpec(memory_space=pltpu.SMEM)]
        + [pl.BlockSpec(memory_space=pltpu.VMEM)] * len(held),
        out_specs=pl.BlockSpec(memory_space=pltpu.VMEM),
        compiler_params=pltpu.CompilerParams(vmem_limit_bytes=VMEM_LIMIT),
    )(table, *held)


def toward(targets, source, only):
    return [
        (device(*source(y, x, c, step), b), device(*only(y, x, c, step), b))
        for b, (y, x, c) in targets.items()
        for step in range(8)
    ]


def copy_kernel(source, out):
    out[...] = source[...]


def placed(value):
    return pl.pallas_call(
        copy_kernel,
        out_shape=pltpu.VMEM(value.shape, value.dtype),
        in_specs=[pl.BlockSpec(memory_space=pltpu.VMEM)],
        out_specs=pl.BlockSpec(memory_space=pltpu.VMEM),
        compiler_params=pltpu.CompilerParams(vmem_limit_bytes=VMEM_LIMIT),
    )(value)


def one_core(value, targets):
    def at(core_of):
        return lambda y, x, c, step: (step // NX, x + step % NX, core_of(c))

    return value + send(value, toward(targets, at(lambda c: 1 - c), at(lambda c: c)))


def along(targets, offset_from, offset_to):
    def at(offset):
        return lambda y, x, c, step: (step % 2, x + offset, c)

    return sorted(set(toward(targets, at(offset_from), at(offset_to))))


def one_x(value, targets):
    parts = [send(value, along(targets, offset, 0)) for offset in (2, 1, 3)]
    return value + parts[0] + (parts[1] + parts[2])


Y_SWAP = every(lambda y, x, c, h, z: (1 - y, x, c, block(h, z)))
CORE_SWAP = every(lambda y, x, c, h, z: (y, x, 1 - c, block(h, z)))
FROM_LEFT = every(lambda y, x, c, h, z: (y, x - 1, c, block(h, z)))
FROM_FAR = every(lambda y, x, c, h, z: (y, x + 2, c, block(h, z)))
FROM_RIGHT = every(lambda y, x, c, h, z: (y, x + 1, c, block(h, z)))
FROM_UP = every(lambda y, x, c, h, z: (y, x, c, block(h, z + 1)))
FROM_DOWN = every(lambda y, x, c, h, z: (y, x, c, block(h, z - 1)))
FROM_OTHER = every(lambda y, x, c, h, z: (y, x, c, block(h + 1, z)))


def near(keep, got):
    middle = keep.shape[1] // 2
    far_top = send(keep[2, :middle] + got[2, :middle], FROM_LEFT)
    far_bottom = send(keep[2, middle:] + got[2, middle:], FROM_RIGHT)
    right = keep[1] + got[1]
    right = jnp.concatenate([right[:middle] + far_top, right[middle:]], 0)
    left = keep[3] + got[3]
    left = jnp.concatenate([left[:middle], left[middle:] + far_bottom], 0)
    return keep[0] + got[0], right, left


def split(value):
    return [value[j] for j in range(NX)]


def together(*values):
    return lax.optimization_barrier(values)


def per_device(half_b):
    local, codes_c, target_c, first, halves, final, final_c = plan()
    aux, blk = lax.axis_index("aux"), lax.axis_index("blk")
    place = aux * GROUPS + blk
    table_a, table_b = jnp.asarray(local[0])[place], jnp.asarray(local[1])[place]
    table_c = jnp.asarray(codes_c)[blk]

    held = {O: placed(half_b)}
    held[PZ] = send(half_b, FROM_UP)
    held[MZ] = send(half_b, FROM_DOWN)
    held[Y0] = send(half_b, FROM_OTHER)
    held[O], held[PZ], held[MZ], held[Y0] = together(held[O], held[PZ], held[MZ], held[Y0])

    held[PP] = send(held[PZ], FROM_UP)
    held[MM] = send(held[MZ], FROM_DOWN)
    held[Y1] = send(held[PZ], FROM_OTHER)
    given, keep = (products(table_a, [held[n] for n in HELD_A], HELD_A, PAIRS_A, kept) for kept in (0, 1))
    own_a, right_a, left_a = near(keep, send(given, CORE_SWAP))
    total_a = own_a + send(right_a, FROM_LEFT) + send(left_a, FROM_RIGHT)
    total_a, held[PP], held[MM], held[Y1] = together(total_a, held[PP], held[MM], held[Y1])

    held[Y2] = send(held[PP], FROM_OTHER)
    given, keep = (products(table_b, [held[n] for n in HELD_B], HELD_B, PAIRS_B, kept) for kept in (0, 1))
    own, *others = together(*(k + g for k, g in zip(split(keep), split(send(given, CORE_SWAP)))))
    right, far, left = (send(part, pairs) for part, pairs in zip(others, (FROM_LEFT, FROM_FAR, FROM_RIGHT)))
    held[Y2], right = together(held[Y2], right)
    part_c = products(table_c, [held[n] for n in HELD_C], HELD_C, PAIRS_C, 1, 1)
    part_c = one_core(part_c[0], target_c)
    total_b, part_c = together((own + right) + (far + left), part_c)

    has_first = jnp.asarray(first)[aux, blk]
    done = jnp.where(has_first, total_a, total_b) + send(jnp.where(has_first, total_b, total_a), Y_SWAP)
    part_c = one_x(part_c, target_c)
    done, part_c = together(done, part_c)

    own_half = jnp.asarray(halves)[aux, blk]
    top = send(jnp.where(own_half == 0, done, part_c), final[0]) + send(part_c, final_c[0])
    bottom = send(jnp.where(own_half == 1, done, part_c), final[1]) + send(part_c, final_c[1])
    return jnp.concatenate([top, bottom], 0)


def solution(mesh):
    placed = (P("aux", "blk", None),)
    return jax.shard_map(
        per_device, mesh=mesh, in_specs=placed, out_specs=P("blk", "aux"), check_vma=False
    )
```

```python
import collections
import functools
import random

import jax
import jax.numpy as jnp
import numpy as np
from jax import lax
from jax.experimental import pallas as pl
from jax.experimental.pallas import tpu as pltpu
from jax.sharding import PartitionSpec as P

ALL = ("aux", "blk")
NX, NZ, GROUPS = 4, 8, 16
VMEM_LIMIT = 16 * 2**20


def device(y_lo, x, core, blk):
    return ((y_lo * NX + x % NX) * 2 + core) * GROUPS + blk


def block(h, z):
    return h % 2 * NZ + z % NZ


def every(move):
    return [
        (device(*move(y_lo, x, core, h, z)), device(y_lo, x, core, block(h, z)))
        for y_lo in range(2)
        for x in range(NX)
        for core in range(2)
        for h in range(2)
        for z in range(NZ)
    ]


def send(value, pairs):
    return lax.ppermute(value, ALL, pairs)


O, PZ, MZ, Y0 = (0, 0), (0, 1), (0, -1), (1, 0)
PP, MM, Y1, Y2 = (0, 2), (0, -2), (1, 1), (1, 2)
HELD_A = (O, PZ, MZ, Y0)
HELD_B = (O, MZ, PP, MM, Y1)
HELD_C = (MM, Y2)


def units_of(pairs, h, z):
    found = []
    for at, (first, second, halves) in enumerate(pairs):
        i, j = block(h + first[0], z + first[1]), block(h + second[0], z + second[1])
        for half in halves(h, z):
            core = half if halves is both else int(first == second)
            found.append(((at, int(i > j), core), min(i, j), max(i, j), half))
    return found


def both(h, z):
    return (0, 1)


def by_h(h, z):
    return (h,)


def by_z(h, z):
    return (0,) if 2 <= z < 6 else (1,)


def upper(h, z):
    return (0,)


def lower(h, z):
    return (1,)


PAIRS_A = ((O, PZ, both), (MZ, PZ, both), (O, Y0, by_h), (MZ, Y0, both), (O, O, upper))
PAIRS_B = ((MZ, PP, both), (MM, PP, by_z), (MZ, Y1, both), (MM, Y1, both), (O, O, lower))
PAIRS_C = ((MM, Y2, by_h),)


def steps(a, b, n):
    ahead, back = (b - a) % n, (a - b) % n
    found = []
    if ahead and ahead <= back:
        found += [((a + i) % n, 1, 1.0) for i in range(ahead)]
    if ahead and back <= ahead:
        found += [((a - i) % n, -1, 1.0) for i in range(back)]
    return found


@functools.cache
def route(source, target):
    found = []
    for weight, order in ((1.0, (2, 0, 1)), (0.01, (2, 1, 0))):
        at = list(source)
        for axis in order:
            for place, way, share in steps(at[axis], target[axis], (NX, 4, NZ)[axis]):
                link = at[:axis] + [place] + at[axis + 1 :]
                found.append(((weight, axis, way, *link), share))
            at[axis] = target[axis]
    return found


def links(own, place, y, unit):
    h, z = own // NZ, own % NZ
    _, row, col, _ = unit
    return route((place // 2, 2 * h + y, z), (col // 2 % NX, row // NZ * 2 + col // NZ, row % NZ))


def by_core(units):
    cores = [[index for index, unit in enumerate(units) if unit[0][2] == core] for core in (0, 1)]
    return [cores[place % 2][place // 2] for place in range(8)]


@functools.cache
def spread(trials=120000):
    draw = random.Random(0)
    where = [(own // NZ, own % NZ) for own in range(GROUPS)]
    units = [[units_of(pairs, h, z) for pairs in (PAIRS_A, PAIRS_B)] for h, z in where]
    at = [[by_core(batch) for batch in both_batches] for both_batches in units]
    planes = [[h] * 8 for h, _ in where]
    load = collections.Counter()

    def on(own, batch, place, index, y):
        return links(own, place, 1 - y if batch else y, units[own][batch][index])

    for own, (h, z) in enumerate(where):
        for batch in (0, 1):
            for place in range(8):
                for link, share in on(own, batch, place, at[own][batch][place], planes[own][place]):
                    load[link] += share
        for unit in units_of(PAIRS_C, h, z):
            for y in (0, 1):
                for link, share in links(own, unit[2] % 8, y, unit):
                    load[link] += 3 * share
    for _ in range(trials):
        own, batch, u, v = draw.randrange(GROUPS), draw.randrange(2), draw.randrange(8), draw.randrange(8)
        if (u - v) % 2:
            continue
        now, plane = at[own], planes[own]
        change = collections.Counter()
        if u == v:
            for one in (0, 1):
                for sign, y in ((-1, plane[u]), (1, 1 - plane[u])):
                    for link, share in on(own, one, u, now[one][u], y):
                        change[link] += sign * share
        else:
            i, j = now[batch][u], now[batch][v]
            for sign, place, index in ((-1, u, i), (-1, v, j), (1, u, j), (1, v, i)):
                for link, share in on(own, batch, place, index, plane[place]):
                    change[link] += sign * share
        if sum(link[0] * ((load[link] + d) ** 6 - load[link] ** 6) for link, d in change.items()) <= 0:
            for link, d in change.items():
                load[link] += d
            if u == v:
                plane[u] = 1 - plane[u]
            else:
                now[batch][u], now[batch][v] = j, i
    return units, at, planes


@functools.cache
def plan():
    tables = np.zeros((2, 16, GROUPS, 5, 4), np.int32)
    table_c = np.zeros((GROUPS, 4), np.int32)
    target_c = {}
    final = {half: [] for half in (0, 1)}
    final_c = {half: [] for half in (0, 1)}
    halves = np.zeros((16, GROUPS), np.int32)
    first = np.zeros((16, GROUPS), np.bool_)
    units, at, planes = spread()
    for h in range(2):
        for z in range(NZ):
            own = block(h, z)
            for place in range(8):
                x, core = place // 2, place % 2
                for batch in range(2):
                    (pair, swap, _), row, col, half = units[own][batch][at[own][batch][place]]
                    y = 1 - planes[own][place] if batch else planes[own][place]
                    final[half].append((device(y, x, core, own), col * GROUPS + row))
                    first[(y * NX + x) * 2 + core, own] = not batch
                    halves[(y * NX + x) * 2 + core, own] = half
                    for aux in range(16):
                        entry, offset = tables[batch, aux, own, pair], (x - aux // 2) % NX
                        kept = aux % 2 == core
                        entry[0] = swap
                        if (PAIRS_A, PAIRS_B)[batch][pair][2] is both:
                            entry[1 if kept else 2] = offset
                            entry[3] = aux % 2
                        else:
                            entry[1:] = offset, kept, half
            (((_, swap, _), row, col, half),) = units_of(PAIRS_C, h, z)
            table_c[own] = swap, 0, 1, half
            y, x, core = min(
                ((y, x, core) for y in (0, 1) for x in range(NX) for core in (0, 1)
                 if halves[(y * NX + x) * 2 + core, own] != half),
                key=lambda place: (min((place[1] - col // 2) % NX, (col // 2 - place[1]) % NX), place),
            )
            target_c[own] = (y, x, core)
            final[half].append((device(y, x, core, own), col * GROUPS + row))
            final_c[half].append((device(1 - y, x, core, own), col * GROUPS + row))
    return tables.reshape(2, 16 * GROUPS, 20), table_c, target_c, first, halves, final, final_c


def dot_t(a, b):
    return lax.dot_general(a, b, (((1,), (1,)), ((), ())), preferred_element_type=jnp.float32)


def half_product(rows, cols, half):
    at = pl.ds(pl.multiple_of(half * 256, 256), 256)
    total = dot_t(rows[0, at, :], cols[0])
    for k in range(1, rows.shape[0]):
        total += dot_t(rows[k, at, :], cols[k])
    return total


def units_kernel(pairs, index_pairs, spare, table, *refs):
    held, outs = refs[: len(refs) - spare], refs[len(refs) - spare :]
    for at, ((first, second), (_, _, halves)) in enumerate(zip(index_pairs, pairs)):
        swap, one, two, half = (table[4 * at + i] for i in range(4))
        for turned in range(1 if first == second else 2):
            rows, cols = (held[second], held[first]) if turned else (held[first], held[second])
            if halves is both:

                @pl.when(swap == turned)
                def _():
                    outs[1][two] = half_product(rows, cols, 1 - half)
                    outs[0][one] = half_product(rows, cols, half)

            else:
                for mine in range(2 - len(outs), 2):

                    @pl.when((swap == turned) & (two == mine))
                    def _():
                        outs[1 - mine][one] = half_product(rows, cols, half)


def products(table, held, names, pairs, counts):
    index_pairs = tuple((names.index(a), names.index(b)) for a, b, _ in pairs)
    return pl.pallas_call(
        functools.partial(units_kernel, pairs, index_pairs, len(counts)),
        out_shape=[pltpu.VMEM((count, 256, 512), jnp.float32) for count in counts],
        in_specs=[pl.BlockSpec(memory_space=pltpu.SMEM)]
        + [pl.BlockSpec(memory_space=pltpu.VMEM)] * len(held),
        out_specs=[pl.BlockSpec(memory_space=pltpu.VMEM)] * len(counts),
        compiler_params=pltpu.CompilerParams(vmem_limit_bytes=VMEM_LIMIT),
    )(table, *held)


def toward(targets, source, only):
    return [
        (device(*source(y, x, c, step), b), device(*only(y, x, c, step), b))
        for b, (y, x, c) in targets.items()
        for step in range(8)
    ]


def copy_kernel(source, out):
    out[...] = source[...]


def placed(value):
    return pl.pallas_call(
        copy_kernel,
        out_shape=pltpu.VMEM(value.shape, value.dtype),
        in_specs=[pl.BlockSpec(memory_space=pltpu.VMEM)],
        out_specs=pl.BlockSpec(memory_space=pltpu.VMEM),
        compiler_params=pltpu.CompilerParams(vmem_limit_bytes=VMEM_LIMIT),
    )(value)


def one_core(value, targets):
    def at(core_of):
        return lambda y, x, c, step: (step // NX, x + step % NX, core_of(c))

    return value + send(value, toward(targets, at(lambda c: 1 - c), at(lambda c: c)))


def along(targets, offset_from, offset_to):
    def at(offset):
        return lambda y, x, c, step: (step % 2, x + offset, c)

    return sorted(set(toward(targets, at(offset_from), at(offset_to))))


def one_x(value, targets):
    parts = [send(value, along(targets, offset, 0)) for offset in (2, 1, 3)]
    return value + parts[0] + (parts[1] + parts[2])


Y_SWAP = every(lambda y, x, c, h, z: (1 - y, x, c, block(h, z)))
CORE_SWAP = every(lambda y, x, c, h, z: (y, x, 1 - c, block(h, z)))
FROM_LEFT = every(lambda y, x, c, h, z: (y, x - 1, c, block(h, z)))
FROM_FAR = every(lambda y, x, c, h, z: (y, x + 2, c, block(h, z)))
FROM_RIGHT = every(lambda y, x, c, h, z: (y, x + 1, c, block(h, z)))
FROM_UP = every(lambda y, x, c, h, z: (y, x, c, block(h, z + 1)))
FROM_DOWN = every(lambda y, x, c, h, z: (y, x, c, block(h, z - 1)))
FROM_OTHER = every(lambda y, x, c, h, z: (y, x, c, block(h + 1, z)))


def near(keep, got):
    middle = keep.shape[1] // 2
    far_top = send(keep[2, :middle] + got[2, :middle], FROM_LEFT)
    far_bottom = send(keep[2, middle:] + got[2, middle:], FROM_RIGHT)
    right = keep[1] + got[1]
    right = jnp.concatenate([right[:middle] + far_top, right[middle:]], 0)
    left = keep[3] + got[3]
    left = jnp.concatenate([left[:middle], left[middle:] + far_bottom], 0)
    return keep[0] + got[0], right, left


def split(value):
    return [value[j] for j in range(NX)]


def together(*values):
    return lax.optimization_barrier(values)


def per_device(half_b):
    local, codes_c, target_c, first, halves, final, final_c = plan()
    aux, blk = lax.axis_index("aux"), lax.axis_index("blk")
    place = aux * GROUPS + blk
    table_a, table_b = jnp.asarray(local[0])[place], jnp.asarray(local[1])[place]
    table_c = jnp.asarray(codes_c)[blk]

    held = {O: placed(half_b)}
    held[PZ] = send(half_b, FROM_UP)
    held[MZ] = send(half_b, FROM_DOWN)
    held[Y0] = send(half_b, FROM_OTHER)
    held[O], held[PZ], held[MZ], held[Y0] = together(held[O], held[PZ], held[MZ], held[Y0])

    held[PP] = send(held[PZ], FROM_UP)
    held[MM] = send(held[MZ], FROM_DOWN)
    held[Y1] = send(held[PZ], FROM_OTHER)
    keep, given = products(table_a, [held[n] for n in HELD_A], HELD_A, PAIRS_A, (NX, NX))
    own_a, right_a, left_a = near(keep, send(given, CORE_SWAP))
    total_a = own_a + send(right_a, FROM_LEFT) + send(left_a, FROM_RIGHT)
    total_a, held[PP], held[MM], held[Y1] = together(total_a, held[PP], held[MM], held[Y1])

    held[Y2] = send(held[PP], FROM_OTHER)
    keep, given = products(table_b, [held[n] for n in HELD_B], HELD_B, PAIRS_B, (NX, NX))
    own, *others = together(*(k + g for k, g in zip(split(keep), split(send(given, CORE_SWAP)))))
    right, far, left = (send(part, pairs) for part, pairs in zip(others, (FROM_LEFT, FROM_FAR, FROM_RIGHT)))
    held[Y2], right = together(held[Y2], right)
    (part_c,) = products(table_c, [held[n] for n in HELD_C], HELD_C, PAIRS_C, (1,))
    part_c = one_core(part_c[0], target_c)
    total_b, part_c = together((own + right) + (far + left), part_c)

    has_first = jnp.asarray(first)[aux, blk]
    done = jnp.where(has_first, total_a, total_b) + send(jnp.where(has_first, total_b, total_a), Y_SWAP)
    part_c = one_x(part_c, target_c)
    done, part_c = together(done, part_c)

    own_half = jnp.asarray(halves)[aux, blk]
    top = send(jnp.where(own_half == 0, done, part_c), final[0]) + send(part_c, final_c[0])
    bottom = send(jnp.where(own_half == 1, done, part_c), final[1]) + send(part_c, final_c[1])
    return jnp.concatenate([top, bottom], 0)


def solution(mesh):
    placed = (P("aux", "blk", None),)
    return jax.shard_map(
        per_device, mesh=mesh, in_specs=placed, out_specs=P("blk", "aux"), check_vma=False
    )
```
